32 devices in a mesh: tm: 2 (over y), space: 16 (over z, x, core).
Axes of the slice: x: 2, y: 2, z: 4, core: 2. Of those that a mesh axis runs over, the one named last changes fastest.
Arguments:
- image: float32 [2, 2, 2560, 128], P(None, 'tm', 'space'), may hold values from -6 to 6
- extrap: float32 [2, 2, 2560, 128], P(None, 'tm', 'space'), may hold values from -6 to 6
- tv_dual: float32 [2, 2, 2560, 128], P(None, 'tm', 'space'), may hold values from -1 to 1
- data_dual: float32 [2, 2, 16, 16, 160, 128], P(None, 'tm', 'space'), may hold values from -4 to 4
- kspace: float32 [2, 2, 16, 16, 160, 128], P(None, 'tm', 'space'), may hold values from -6 to 6
- coil_maps: float32 [2, 16, 2560, 128], P(None, 'space'), may hold values from -1 to 1
- sampling: int32 [2, 160, 128], P('tm'), may hold values 0 or 1
Outputs:
- image_new: float32 [2, 2, 2560, 128], P(None, 'tm', 'space')
- tv_new: float32 [2, 2, 2560, 128], P(None, 'tm', 'space')
- data_new: float32 [2, 2, 16, 16, 160, 128], P(None, 'tm', 'space')
The draws below stay inside these ranges and needn't reach their ends.
All inputs are finite; a program needn't handle non-finite values. No bound on the sum of `sampling` on one device may be relied on, other than what follows from the above.
Results may differ from the reference program's by a relative error of at most 0.000061.
Values sent between devices are 32-bit elements; how exact they have to be, the bound alone decides.
No kernel may reach another device: no remote copies, remote signals or barrier semaphores. Data moves between devices by JAX's collectives and lax.ppermute only.
A program may use at most 64 MiB of HBM per device.

```python
import jax
import jax.numpy as jnp
from jax import lax

NY = 160
NZ = 128
X = 16
COILS = 16
FRAMES = 2


def touch_ends(result, stream_key, smallest, high):
    longest = result.shape.index(max(result.shape))
    spots = []
    for shift in (0, 1):
        where = [jax.random.randint(jax.random.fold_in(stream_key, axis), (), 0, length) for axis, length in enumerate(result.shape)]
        where[longest] = (where[longest] + shift) % result.shape[longest]
        spots.append(tuple(where))
    return result.at[spots[0]].set(smallest).at[spots[1]].set(high)


def level_of(key, shape, shards, low, top_value):
    loudness = 1.0
    for position, parts in shards:
        draws = jax.random.uniform(jax.random.fold_in(jax.random.fold_in(key, 6), position), (parts,), jnp.float32, low / len(shards), top_value / len(shards))
        loudness = loudness * jnp.repeat(jnp.exp(draws), shape[position] // parts).reshape((-1,) + (1,) * (len(shape) - 1 - position))
    return loudness


def gaussian(rng, shape, deviation, bound, shards=(), held_as=jnp.bfloat16):
    drawn = jax.random.normal(rng, shape, jnp.float32) * deviation
    if len(shards) > 0:
        drawn = level_of(rng, shape, shards, -0.22, 0.18) * drawn
    return jnp.clip(drawn, min=-bound, max=bound).astype(held_as)


def setup_inputs(seed: int = 0) -> dict:
    arg_keys = jax.random.split(jax.random.key(seed), 8)
    image = gaussian(arg_keys[0], (2, FRAMES, X * NY, NZ), 1.0, 6.0, ((1, 2), (2, 16)), jnp.float32)
    extrap = gaussian(arg_keys[1], (2, FRAMES, X * NY, NZ), 1.0, 6.0, ((1, 2), (2, 16)), jnp.float32)
    tv_dual = gaussian(arg_keys[2], (2, FRAMES, X * NY, NZ), 0.2, 1.0, ((1, 2), (2, 16)), jnp.float32)
    data_dual = gaussian(arg_keys[3], (2, FRAMES, COILS, X, NY, NZ), 0.5, 4.0, ((1, 2), (2, 16)), jnp.float32)
    kspace = gaussian(arg_keys[4], (2, FRAMES, COILS, X, NY, NZ), 1.0, 6.0, ((1, 2), (2, 16)), jnp.float32)
    coil_maps = gaussian(arg_keys[5], (2, COILS, X * NY, NZ), (2 * COILS) ** -0.5, 1.0, ((1, 16),), jnp.float32)
    sampling = touch_ends((jax.random.randint(arg_keys[6], (FRAMES, NY, NZ), 0, 5) < 2).astype(jnp.int32), jax.random.fold_in(arg_keys[6], 1), 0, 1)
    return dict(image=image, extrap=extrap, tv_dual=tv_dual, data_dual=data_dual, kspace=kspace, coil_maps=coil_maps, sampling=sampling)


dual_step = 0.4
primal_step = 0.4
clip_level = 0.5

def project(real_part, imag_part):
    magnitude = jnp.sqrt(real_part * real_part + imag_part * imag_part)
    factor = clip_level / jnp.maximum(magnitude, clip_level)
    return (real_part * factor, imag_part * factor)

def reference(image, extrap, tv_dual, data_dual, kspace, coil_maps, sampling):
    frames = image.shape[1]
    later = jnp.concatenate([extrap[:, 1:], jnp.zeros_like(extrap[:, :1])], axis=1)
    keeps = (jnp.arange(frames) < frames - 1).astype(image.dtype)[None, :, None, None]
    moved = tv_dual + dual_step * keeps * (later - extrap)
    new_real, new_imag = project(moved[0], moved[1])
    tv_new = jnp.stack([new_real, new_imag])
    earlier = jnp.concatenate([jnp.zeros_like(tv_new[:, :1]), tv_new[:, :-1]], axis=1)
    temporal = earlier - keeps * tv_new
    maps = (coil_maps[0] + 1j * coil_maps[1]).reshape(COILS, X, NY, NZ)

    def one_frame(inputs):
        frame_image, frame_dual, frame_data, frame_mask = inputs
        volume = (frame_image[0] + 1j * frame_image[1]).reshape(X, NY, NZ)
        spectrum = jnp.fft.fft2(maps * volume[None], axes=(-2, -1), norm='ortho')
        measured = frame_data[0] + 1j * frame_data[1]
        previous = frame_dual[0] + 1j * frame_dual[1]
        weight = frame_mask.astype(image.dtype)
        updated = weight * (previous + dual_step * (spectrum - measured)) / (1.0 + dual_step)
        back = lax.optimization_barrier(jnp.sum(jnp.conj(maps) * jnp.fft.ifft2(updated, axes=(-2, -1), norm='ortho'), axis=0))
        back = back.reshape(X * NY, NZ)
        updated_pair = jnp.stack([updated.real, updated.imag]).astype(image.dtype)
        back_pair = jnp.stack([back.real, back.imag]).astype(image.dtype)
        return (updated_pair, back_pair)
    data_new, adjoint = lax.map(one_frame, (jnp.moveaxis(extrap, 1, 0), jnp.moveaxis(data_dual, 1, 0), jnp.moveaxis(kspace, 1, 0), sampling))
    data_new = jnp.moveaxis(data_new, 0, 1)
    adjoint = jnp.moveaxis(adjoint, 0, 1)
    image_new = image - primal_step * (adjoint + temporal)
    return (image_new, tv_new, data_new)
```

```python
import functools
import math

import jax
import jax.numpy as jnp
import ml_dtypes
import numpy as np
from jax import lax
from jax.experimental import pallas as pl
from jax.experimental.pallas import tpu as pltpu
from jax.sharding import PartitionSpec as P

dual_step = 0.4
primal_step = 0.4
clip_level = 0.5


def split_host(table):
    high = table.astype(ml_dtypes.bfloat16)
    low = (table - high.astype(np.float64)).astype(ml_dtypes.bfloat16)
    return high, low


def column_table(length, sign):
    places = np.arange(length)
    angles = 2.0 * math.pi * (np.outer(places, places) % length) / length
    real = np.cos(angles) / math.sqrt(length)
    imag = sign * np.sin(angles) / math.sqrt(length)
    whole = np.block([[real, imag], [-imag, real]])
    high, low = split_host(whole)
    return np.concatenate([high, high, low], axis=0)


def row_tables(length, sign):
    half = length // 2
    found = []
    for odd in (0, 1):
        lines = np.arange(half)
        cells = 2 * np.arange(half) + odd
        product = np.outer(lines, cells)
        angles = 2.0 * math.pi * (product % length) / length
        real = np.cos(angles) / math.sqrt(length)
        imag = sign * np.sin(angles) / math.sqrt(length)
        if sign > 0:
            real, imag = real.T, imag.T
        whole = np.block([[real, -imag], [imag, real]])
        high, low = split_host(whole)
        found.append(np.concatenate([high, high, low], axis=1))
    return found


def split(values):
    high = values.astype(jnp.bfloat16)
    low = (values - high.astype(jnp.float32)).astype(jnp.bfloat16)
    return high, low


def columns_dft(real, imag, table):
    real_high, real_low = split(real)
    imag_high, imag_low = split(imag)
    left = jnp.concatenate([real_high, imag_high, real_low, imag_low, real_high, imag_high], axis=1)
    return jnp.dot(left, table, preferred_element_type=jnp.float32)


def rows_dft(table, values):
    high, low = split(values)
    return jnp.dot(table, jnp.concatenate([high, low, high], axis=0), preferred_element_type=jnp.float32)


def coil_kernel(offsets, chained, *refs):
    count = len(offsets)
    place, refs = refs[0], refs[1:]
    mine, theirs, refs = refs[:count], refs[count:2 * count], refs[2 * count:]
    coil, dual, kspace, mask = refs[:4]
    col_fwd, even_fwd, odd_fwd, col_bwd, even_bwd, odd_bwd = refs[4:10]
    refs = refs[10 + chained:]
    keep, give, data_new = refs[:3]
    coil_buf, dual_buf, ksp_buf, new_buf, u_buf, v_buf, weight, in_sem, out_sem = refs[3:]
    own = mine[0].shape[1]
    rows = 2 * own
    height = mask.shape[1]
    half = height // 2
    planes = rows // height
    core = place[1]
    at = [pl.multiple_of(core * own, own), pl.multiple_of((1 - core) * own, own)]

    loads = []
    for n, offset in enumerate(offsets):
        chip = jnp.bitwise_xor(place[0], offset)
        row0 = pl.multiple_of(chip * rows, rows)
        plane0 = chip * planes
        loads.append([
            pltpu.make_async_copy(coil.at[:, 0, pl.ds(row0, rows), :], coil_buf.at[n], in_sem.at[n, 0]),
            pltpu.make_async_copy(dual.at[:, 0, 0, pl.ds(plane0, planes)], dual_buf.at[n], in_sem.at[n, 1]),
            pltpu.make_async_copy(kspace.at[:, 0, 0, pl.ds(plane0, planes)], ksp_buf.at[n], in_sem.at[n, 2]),
        ])
        for load in loads[-1]:
            load.start()
    weight[...] = mask[0].astype(jnp.float32) / (1.0 + dual_step)

    stores = []
    for n, offset in enumerate(offsets):
        loads[n][0].wait()
        parts = []
        for block, start in zip((mine[n], theirs[n]), at):
            map_re = coil_buf[n, 0, pl.ds(start, own), :]
            map_im = coil_buf[n, 1, pl.ds(start, own), :]
            parts.append((map_re * block[0] - map_im * block[1], map_re * block[1] + map_im * block[0]))
        lines = columns_dft(
            jnp.concatenate([parts[0][0], parts[1][0]], axis=0),
            jnp.concatenate([parts[0][1], parts[1][1]], axis=0),
            col_fwd[...],
        )
        depth = lines.shape[1] // 2
        for part, start in enumerate(at):
            u_buf[0, pl.ds(start, own), :] = lines[part * own:(part + 1) * own, :depth]
            u_buf[1, pl.ds(start, own), :] = lines[part * own:(part + 1) * own, depth:]
        halves = []
        for odd, table in ((0, even_fwd), (1, odd_fwd)):
            cells = jnp.concatenate([
                jnp.concatenate([u_buf[part, pl.ds(p * height + odd, half, stride=2), :] for part in (0, 1)], axis=0)
                for p in range(planes)
            ], axis=1)
            halves.append(rows_dft(table[...], cells))
        loads[n][1].wait()
        loads[n][2].wait()
        spectrum = (halves[0] + halves[1], halves[0] - halves[1])
        updated = []
        for q in (0, 1):
            span = pl.ds(q * half, half)
            columns = []
            for p in range(planes):
                pieces = []
                for part in (0, 1):
                    value = spectrum[q][part * half:(part + 1) * half, p * depth:(p + 1) * depth]
                    new = weight[span, :] * (
                        dual_buf[n, part, p, span, :] + dual_step * (value - ksp_buf[n, part, p, span, :])
                    )
                    new_buf[n, part, p, span, :] = new
                    pieces.append(new)
                columns.append(jnp.concatenate(pieces, axis=0))
            updated.append(jnp.concatenate(columns, axis=1))
        chip = jnp.bitwise_xor(place[0], offset)
        store = pltpu.make_async_copy(
            new_buf.at[n], data_new.at[:, 0, 0, pl.ds(chip * planes, planes)], out_sem.at[n]
        )
        store.start()
        stores.append(store)
        for odd, table in ((0, even_bwd), (1, odd_bwd)):
            back = rows_dft(table[...], updated[0] - updated[1] if odd else updated[0] + updated[1])
            for p in range(planes):
                for part in (0, 1):
                    v_buf[part, pl.ds(p * height + odd, half, stride=2), :] = back[
                        part * half:(part + 1) * half, p * depth:(p + 1) * depth
                    ]
        plane = columns_dft(
            jnp.concatenate([v_buf[0, pl.ds(start, own), :] for start in at], axis=0),
            jnp.concatenate([v_buf[1, pl.ds(start, own), :] for start in at], axis=0),
            col_bwd[...],
        )
        for part, (target, start) in enumerate(zip((keep, give), at)):
            map_re = coil_buf[n, 0, pl.ds(start, own), :]
            map_im = coil_buf[n, 1, pl.ds(start, own), :]
            back_re = plane[part * own:(part + 1) * own, :depth]
            back_im = plane[part * own:(part + 1) * own, depth:]
            target[n, 0] = map_re * back_re + map_im * back_im
            target[n, 1] = map_re * back_im - map_im * back_re
    for store in stores:
        store.wait()


def coil_terms(offsets, place, mine, theirs, coil, dual, kspace, mask, constants, previous):
    count = len(offsets)
    own, depth = mine[0].shape[1:]
    height = mask.shape[1]
    planes = 2 * own // height
    vmem = pl.BlockSpec(memory_space=pltpu.VMEM)
    anywhere = pl.BlockSpec(memory_space=pl.ANY)
    operands = [place, *mine, *theirs, coil, dual, kspace, mask, *constants]
    in_specs = (
        [pl.BlockSpec(memory_space=pltpu.SMEM)] + [vmem] * (2 * count) + [anywhere] * 3 + [vmem] * 7
    )
    aliases = {}
    if previous is not None:
        aliases = {len(operands): 2}
        operands.append(previous)
        in_specs.append(anywhere)
    block = (count, 2, own, depth)
    planes_shape = (count, 2, planes, height, depth)
    return pl.pallas_call(
        functools.partial(coil_kernel, offsets, previous is not None),
        out_shape=[
            jax.ShapeDtypeStruct(block, jnp.float32),
            jax.ShapeDtypeStruct(block, jnp.float32),
            jax.ShapeDtypeStruct(dual.shape, jnp.float32),
        ],
        in_specs=in_specs,
        out_specs=[vmem, vmem, anywhere],
        scratch_shapes=[
            pltpu.VMEM((count, 2, 2 * own, depth), jnp.float32),
            pltpu.VMEM(planes_shape, jnp.float32),
            pltpu.VMEM(planes_shape, jnp.float32),
            pltpu.VMEM(planes_shape, jnp.float32),
            pltpu.VMEM((2, 2 * own, depth), jnp.float32),
            pltpu.VMEM((2, 2 * own, depth), jnp.float32),
            pltpu.VMEM((height, depth), jnp.float32),
            pltpu.SemaphoreType.DMA((count, 3)),
            pltpu.SemaphoreType.DMA((count,)),
        ],
        input_output_aliases=aliases,
        compiler_params=pltpu.CompilerParams(vmem_limit_bytes=24 * 1024 * 1024),
        cost_estimate=pl.CostEstimate(
            flops=count * 200_000_000, bytes_accessed=count * 1_400_000, transcendentals=0
        ),
    )(*operands)


def passed_along(value, axis, steps):
    count = lax.axis_size(axis)
    initial, last = (max(0, -steps), min(count, count - steps))
    return lax.ppermute(value, axis, [(source, source + steps) for source in range(initial, last)])


def project(real_part, imag_part):
    magnitude = jnp.sqrt(real_part * real_part + imag_part * imag_part)
    factor = clip_level / jnp.maximum(magnitude, clip_level)
    return (real_part * factor, imag_part * factor)


def swapped(value, mask):
    count = lax.axis_size("space")
    return lax.ppermute(value, "space", [(source, source ^ mask) for source in range(count)])


def on_device(image, extrap, tv_dual, data_dual, kspace, coil_maps, sampling):
    height, depth = kspace.shape[4:]
    chips = lax.axis_size("space") // 2
    inner = chips // 4
    here = lax.axis_index("space")
    place = jnp.stack([here // 2, here % 2]).astype(jnp.int32)
    constants = [
        jnp.asarray(table)
        for table in (
            column_table(depth, -1), *row_tables(height, -1), column_table(depth, 1), *row_tables(height, 1)
        )
    ]
    frame_here = lax.axis_index("tm")
    frame_total = lax.axis_size("tm")
    not_last = (frame_here < frame_total - 1).astype(jnp.float32)
    current = extrap[:, 0]

    mine = {0: current}
    for z in (2, 3):
        mine[z * inner] = swapped(current, 2 * z * inner)
    for i in range(1, inner):
        mine[i] = swapped(current, 2 * i)
    for i in range(inner):
        mine[inner + i] = swapped(mine[i], 2 * inner)
    for z in (2, 3):
        for i in range(1, inner):
            mine[z * inner + i] = swapped(mine[z * inner], 2 * i)
    theirs = {offset: swapped(block, 1) for offset, block in mine.items()}

    near = tuple(range(2 * inner))
    far = tuple(range(2 * inner, 4 * inner))
    sums = {}
    data_new = None
    for offsets in (near, far):
        keep, give, data_new = coil_terms(
            offsets, place, [mine[o] for o in offsets], [theirs[o] for o in offsets],
            coil_maps, data_dual, kspace, sampling, constants, data_new,
        )
        both = keep + swapped(give, 1)
        for n, offset in enumerate(offsets):
            sums[offset] = both[n]

    adjoint = sums[0]
    for z in (2, 3):
        term = sums[z * inner]
        for i in range(1, inner):
            term = term + swapped(sums[z * inner + i], 2 * i)
        adjoint = adjoint + swapped(term, 2 * z * inner)
    for i in range(inner):
        term = swapped(sums[inner + i], 2 * inner)
        if i:
            term = swapped(term + sums[i], 2 * i)
        adjoint = adjoint + term

    later = passed_along(current, "tm", -1)
    moved = tv_dual[:, 0] + dual_step * not_last * (later - current)
    tv_real, tv_imag = project(moved[0], moved[1])
    tv_here = jnp.stack([tv_real, tv_imag])
    earlier = passed_along(tv_here, "tm", 1)
    temporal = earlier - not_last * tv_here
    image_new = image[:, 0] - primal_step * (adjoint + temporal)
    return (image_new[:, None], tv_here[:, None], data_new)


def solution(mesh):
    in_specs = (
        P(None, "tm", "space", None),
        P(None, "tm", "space", None),
        P(None, "tm", "space", None),
        P(None, "tm", "space", None, None, None),
        P(None, "tm", "space", None, None, None),
        P(None, "space", None, None),
        P("tm", None, None),
    )
    out_specs = (
        P(None, "tm", "space", None),
        P(None, "tm", "space", None),
        P(None, "tm", "space", None, None, None),
    )
    return jax.shard_map(
        on_device, mesh=mesh, in_specs=in_specs, out_specs=out_specs, check_vma=False
    )
```

```python
import functools
import math

import jax
import jax.numpy as jnp
import ml_dtypes
import numpy as np
from jax import lax
from jax.experimental import pallas as pl
from jax.experimental.pallas import tpu as pltpu
from jax.sharding import PartitionSpec as P

dual_step = 0.4
primal_step = 0.4
clip_level = 0.5


def split_host(table):
    high = table.astype(ml_dtypes.bfloat16)
    low = (table - high.astype(np.float64)).astype(ml_dtypes.bfloat16)
    return high, low


def column_table(length, sign):
    places = np.arange(length)
    angles = 2.0 * math.pi * (np.outer(places, places) % length) / length
    real = np.cos(angles) / math.sqrt(length)
    imag = sign * np.sin(angles) / math.sqrt(length)
    whole = np.block([[real, imag], [-imag, real]])
    high, low = split_host(whole)
    return np.concatenate([high, high, low], axis=0)


def row_tables(length, sign):
    half = length // 2
    found = []
    for odd in (0, 1):
        lines = np.arange(half)
        cells = 2 * np.arange(half) + odd
        product = np.outer(lines, cells)
        angles = 2.0 * math.pi * (product % length) / length
        real = np.cos(angles) / math.sqrt(length)
        imag = sign * np.sin(angles) / math.sqrt(length)
        if sign > 0:
            real, imag = real.T, imag.T
        whole = np.block([[real, -imag], [imag, real]])
        high, low = split_host(whole)
        found.append(np.concatenate([high, high, low], axis=1))
    return found


def split(values):
    high = values.astype(jnp.bfloat16)
    low = (values - high.astype(jnp.float32)).astype(jnp.bfloat16)
    return high, low


def columns_dft(real, imag, table):
    real_high, real_low = split(real)
    imag_high, imag_low = split(imag)
    left = jnp.concatenate([real_high, imag_high, real_low, imag_low, real_high, imag_high], axis=1)
    return jnp.dot(left, table, preferred_element_type=jnp.float32)


def rows_dft(table, values):
    high, low = split(values)
    return jnp.dot(table, jnp.concatenate([high, low, high], axis=0), preferred_element_type=jnp.float32)


def load_kernel(place, coil, dual, kspace, mask, coil_out, base, gain, ksp_buf, sem):
    count, _, rows, _ = coil_out.shape
    planes = base.shape[2]
    loads = []
    for offset in range(count):
        chip = jnp.bitwise_xor(place[0], offset)
        row0 = pl.multiple_of(chip * rows, rows)
        loads.append([
            pltpu.make_async_copy(
                dual.at[:, 0, 0, pl.ds(chip * planes, planes)], base.at[offset], sem.at[offset, 0]
            ),
            pltpu.make_async_copy(
                kspace.at[:, 0, 0, pl.ds(chip * planes, planes)], ksp_buf.at[offset], sem.at[offset, 1]
            ),
            pltpu.make_async_copy(
                coil.at[:, 0, pl.ds(row0, rows), :], coil_out.at[offset], sem.at[offset, 2]
            ),
        ])
        for load in loads[-1]:
            load.start()
    weight = mask[0].astype(jnp.float32) / (1.0 + dual_step)
    gain[...] = weight * dual_step
    for offset in range(count):
        loads[offset][0].wait()
        loads[offset][1].wait()
        for part in (0, 1):
            for p in range(planes):
                base[offset, part, p] = weight * (
                    base[offset, part, p] - dual_step * ksp_buf[offset, part, p]
                )
    for offset in range(count):
        loads[offset][2].wait()


def coil_kernel(first, count, passing, place, *refs):
    mine, theirs, refs = refs[:count], refs[count:2 * count], refs[2 * count:]
    coil, base, gain = refs[:3]
    col_fwd, even_fwd, odd_fwd, col_bwd, even_bwd, odd_bwd = refs[3:9]
    keep, give, data_new = refs[9 + passing:12 + passing]
    u_buf, v_buf = refs[-2:]
    own = mine[0].shape[1]
    height, depth = gain.shape
    half = height // 2
    planes = base.shape[2]
    core = place[1]
    at = [pl.multiple_of(core * own, own), pl.multiple_of((1 - core) * own, own)]
    for n in reversed(range(count)):
        parts = []
        for block, start in zip((mine[n], theirs[n]), at):
            map_re = coil[first + n, 0, pl.ds(start, own), :]
            map_im = coil[first + n, 1, pl.ds(start, own), :]
            parts.append((map_re * block[0] - map_im * block[1], map_re * block[1] + map_im * block[0]))
        lines = columns_dft(
            jnp.concatenate([parts[0][0], parts[1][0]], axis=0),
            jnp.concatenate([parts[0][1], parts[1][1]], axis=0),
            col_fwd[...],
        )
        for part, start in enumerate(at):
            u_buf[0, pl.ds(start, own), :] = lines[part * own:(part + 1) * own, :depth]
            u_buf[1, pl.ds(start, own), :] = lines[part * own:(part + 1) * own, depth:]
        halves = []
        for odd, table in ((0, even_fwd), (1, odd_fwd)):
            cells = jnp.concatenate([
                jnp.concatenate([u_buf[part, pl.ds(p * height + odd, half, stride=2), :] for part in (0, 1)], axis=0)
                for p in range(planes)
            ], axis=1)
            halves.append(rows_dft(table[...], cells))
        spectrum = (halves[0] + halves[1], halves[0] - halves[1])
        updated = []
        for q in (0, 1):
            span = pl.ds(q * half, half)
            columns = []
            for p in range(planes):
                pieces = []
                for part in (0, 1):
                    value = spectrum[q][part * half:(part + 1) * half, p * depth:(p + 1) * depth]
                    new = gain[span, :] * value + base[first + n, part, p, span, :]
                    data_new[n, part, p, span, :] = new
                    pieces.append(new)
                columns.append(jnp.concatenate(pieces, axis=0))
            updated.append(jnp.concatenate(columns, axis=1))
        for odd, table in ((0, even_bwd), (1, odd_bwd)):
            back = rows_dft(table[...], updated[0] - updated[1] if odd else updated[0] + updated[1])
            for p in range(planes):
                for part in (0, 1):
                    v_buf[part, pl.ds(p * height + odd, half, stride=2), :] = back[
                        part * half:(part + 1) * half, p * depth:(p + 1) * depth
                    ]
        plane = columns_dft(
            jnp.concatenate([v_buf[0, pl.ds(start, own), :] for start in at], axis=0),
            jnp.concatenate([v_buf[1, pl.ds(start, own), :] for start in at], axis=0),
            col_bwd[...],
        )
        for part, (target, start) in enumerate(zip((keep, give), at)):
            map_re = coil[first + n, 0, pl.ds(start, own), :]
            map_im = coil[first + n, 1, pl.ds(start, own), :]
            back_re = plane[part * own:(part + 1) * own, :depth]
            back_im = plane[part * own:(part + 1) * own, depth:]
            target[n, 0] = map_re * back_re + map_im * back_im
            target[n, 1] = map_re * back_im - map_im * back_re


def store_kernel(place, *refs):
    groups, data_new, sem = refs[:-2], refs[-2], refs[-1]
    count, _, planes = groups[0].shape[:3]
    stores = []
    for g, group in enumerate(groups):
        for n in range(count):
            chip = jnp.bitwise_xor(place[0], g * count + n)
            stores.append(pltpu.make_async_copy(
                group.at[n], data_new.at[:, 0, 0, pl.ds(chip * planes, planes)], sem.at[g * count + n]
            ))
            stores[-1].start()
    for store in stores:
        store.wait()


vmem = pl.BlockSpec(memory_space=pltpu.VMEM)
smem = pl.BlockSpec(memory_space=pltpu.SMEM)
hbm = pl.BlockSpec(memory_space=pltpu.HBM)
anywhere = pl.BlockSpec(memory_space=pl.ANY)
mebi = 1024 * 1024


def load_all(place, chips, own, coil, dual, kspace, mask):
    height, depth = mask.shape[1:]
    planes = 2 * own // height
    return pl.pallas_call(
        load_kernel,
        out_shape=[
            jax.ShapeDtypeStruct((chips, 2, 2 * own, depth), jnp.float32),
            jax.ShapeDtypeStruct((chips, 2, planes, height, depth), jnp.float32),
            jax.ShapeDtypeStruct((height, depth), jnp.float32),
        ],
        in_specs=[smem, hbm, hbm, hbm, vmem],
        out_specs=[vmem, vmem, vmem],
        scratch_shapes=[
            pltpu.VMEM((chips, 2, planes, height, depth), jnp.float32),
            pltpu.SemaphoreType.DMA((chips, 3)),
        ],
        compiler_params=pltpu.CompilerParams(vmem_limit_bytes=46 * mebi),
        cost_estimate=pl.CostEstimate(flops=4_000_000, bytes_accessed=8_000_000, transcendentals=0),
        name="load",
    )(place, coil, dual, kspace, mask)


def coil_terms(first, place, mine, theirs, coil, base, gain, constants, passed):
    count = len(mine)
    operands = [place, *mine, *theirs, coil, base, gain, *constants]
    own, depth = mine[0].shape[1:]
    block = (count, 2, own, depth)
    return pl.pallas_call(
        functools.partial(coil_kernel, first, count, len(passed)),
        out_shape=[
            jax.ShapeDtypeStruct(block, jnp.float32),
            jax.ShapeDtypeStruct(block, jnp.float32),
            jax.ShapeDtypeStruct((count,) + base.shape[1:], jnp.float32),
        ] + [jax.ShapeDtypeStruct(value.shape, value.dtype) for value in passed],
        in_specs=[smem] + [vmem] * (len(operands) - 1) + [anywhere] * len(passed),
        out_specs=[vmem, vmem, vmem] + [anywhere] * len(passed),
        input_output_aliases={len(operands) + n: 3 + n for n in range(len(passed))},
        scratch_shapes=[
            pltpu.VMEM((2, 2 * own, depth), jnp.float32),
            pltpu.VMEM((2, 2 * own, depth), jnp.float32),
        ],
        compiler_params=pltpu.CompilerParams(vmem_limit_bytes=20 * mebi),
        cost_estimate=pl.CostEstimate(
            flops=count * 800_000_000, bytes_accessed=count * 100_000, transcendentals=0
        ),
        name="coils",
    )(*operands, *passed)


def store_all(place, groups, kspace):
    count = len(groups) * groups[0].shape[0]
    return pl.pallas_call(
        store_kernel,
        out_shape=jax.ShapeDtypeStruct(kspace.shape, jnp.float32),
        in_specs=[smem] + [vmem] * len(groups),
        out_specs=hbm,
        scratch_shapes=[pltpu.SemaphoreType.DMA((count,))],
        compiler_params=pltpu.CompilerParams(vmem_limit_bytes=20 * mebi),
        cost_estimate=pl.CostEstimate(flops=0, bytes_accessed=2_600_000, transcendentals=0),
        name="store",
    )(place, *groups)


def turned(value, axis, steps):
    count = lax.axis_size(axis)
    return lax.ppermute(value, axis, [(source, (source + steps) % count) for source in range(count)])


def project(moved):
    magnitude = jnp.sqrt(moved[0] * moved[0] + moved[1] * moved[1])
    return moved * (clip_level / jnp.maximum(magnitude, clip_level))


def swapped(value, mask):
    count = lax.axis_size("space")
    return lax.ppermute(value, "space", [(source, source ^ mask) for source in range(count)])


def on_device(image, extrap, tv_dual, data_dual, kspace, coil_maps, sampling):
    height, depth = kspace.shape[4:]
    chips = lax.axis_size("space") // 2
    inner = chips // 4
    here = lax.axis_index("space")
    place = jnp.stack([here // 2, here % 2]).astype(jnp.int32)
    constants = [
        jnp.asarray(table)
        for table in (
            column_table(depth, -1), *row_tables(height, -1), column_table(depth, 1), *row_tables(height, 1)
        )
    ]
    frame_here = lax.axis_index("tm")
    frame_total = lax.axis_size("tm")
    not_first = (frame_here > 0).astype(jnp.float32)
    not_last = (frame_here < frame_total - 1).astype(jnp.float32)
    current = extrap[:, 0]

    later = turned(current, "tm", -1)
    previous = later if frame_total == 2 else turned(current, "tm", 1)
    dual_before = turned(tv_dual[:, 0], "tm", 1)
    tv_here = project(tv_dual[:, 0] + dual_step * not_last * (later - current))
    earlier = not_first * project(dual_before + dual_step * (current - previous))
    start = image[:, 0] - primal_step * (earlier - not_last * tv_here)

    mine = {0: current}
    mine[2 * inner] = swapped(current, 4 * inner)
    for i in range(1, inner):
        mine[i] = swapped(current, 2 * i)
    mine[inner] = swapped(current, 2 * inner)
    mine[3 * inner] = swapped(mine[2 * inner], 2 * inner)
    for z in (1, 2, 3):
        for i in range(1, inner):
            mine[z * inner + i] = swapped(mine[z * inner], 2 * i)
    theirs = {offset: swapped(block, 1) for offset, block in mine.items()}

    coil, base, gain = load_all(place, chips, current.shape[1], coil_maps, data_dual, kspace, sampling)
    sums = {}
    updated = []
    for z in range(4):
        offsets = [z * inner + i for i in range(inner)]
        keep, give, new, *passed = coil_terms(
            z * inner, place, [mine[o] for o in offsets], [theirs[o] for o in offsets],
            coil, base, gain, constants, [start] if z == 0 else [],
        )
        if passed:
            start, = passed
        sums[z] = keep + swapped(give, 1)
        updated.append(new)
    data_new = store_all(place, updated, kspace)

    adjoint = 0.0
    for z in (3, 2):
        term = sums[z][0]
        for i in range(1, inner):
            term = term + swapped(sums[z][i], 2 * i)
        adjoint = adjoint + swapped(term, 2 * z * inner)
    term = sums[0] + swapped(sums[1], 2 * inner)
    adjoint = adjoint + term[0]
    for i in range(1, inner):
        adjoint = adjoint + swapped(term[i], 2 * i)

    image_new = start - primal_step * adjoint
    return (image_new[:, None], tv_here[:, None], data_new)


def solution(mesh):
    in_specs = (
        P(None, "tm", "space", None),
        P(None, "tm", "space", None),
        P(None, "tm", "space", None),
        P(None, "tm", "space", None, None, None),
        P(None, "tm", "space", None, None, None),
        P(None, "space", None, None),
        P("tm", None, None),
    )
    out_specs = (
        P(None, "tm", "space", None),
        P(None, "tm", "space", None),
        P(None, "tm", "space", None, None, None),
    )
    return jax.shard_map(
        on_device, mesh=mesh, in_specs=in_specs, out_specs=out_specs, check_vma=False
    )
```

```python
import functools
import math

import jax
import jax.numpy as jnp
import ml_dtypes
import numpy as np
from jax import lax
from jax.experimental import pallas as pl
from jax.experimental.pallas import tpu as pltpu
from jax.sharding import PartitionSpec as P

dual_step = 0.4
primal_step = 0.4
clip_level = 0.5


def split_host(table):
    high = table.astype(ml_dtypes.bfloat16)
    low = (table - high.astype(np.float64)).astype(ml_dtypes.bfloat16)
    return high, low


def column_table(length, sign):
    places = np.arange(length)
    angles = 2.0 * math.pi * (np.outer(places, places) % length) / length
    real = np.cos(angles) / math.sqrt(length)
    imag = sign * np.sin(angles) / math.sqrt(length)
    whole = np.block([[real, imag], [-imag, real]])
    high, low = split_host(whole)
    return np.concatenate([high, high, low], axis=0)


def row_tables(length, sign):
    half = length // 2
    found = []
    for odd in (0, 1):
        lines = np.arange(half)
        cells = 2 * np.arange(half) + odd
        product = np.outer(lines, cells)
        angles = 2.0 * math.pi * (product % length) / length
        real = np.cos(angles) / math.sqrt(length)
        imag = sign * np.sin(angles) / math.sqrt(length)
        if sign > 0:
            real, imag = real.T, imag.T
        whole = np.block([[real, -imag], [imag, real]])
        high, low = split_host(whole)
        found.append(np.concatenate([high, high, low], axis=1))
    return found


def split(values):
    high = values.astype(jnp.bfloat16)
    low = (values - high.astype(jnp.float32)).astype(jnp.bfloat16)
    return high, low


def columns_dft(real, imag, table):
    real_high, real_low = split(real)
    imag_high, imag_low = split(imag)
    left = jnp.concatenate([real_high, imag_high, real_low, imag_low, real_high, imag_high], axis=1)
    return jnp.dot(left, table, preferred_element_type=jnp.float32)


def rows_dft(table, values):
    high, low = split(values)
    return jnp.dot(table, jnp.concatenate([high, low, high], axis=0), preferred_element_type=jnp.float32)


vmem = pl.BlockSpec(memory_space=pltpu.VMEM)
hbm = pl.BlockSpec(memory_space=pltpu.HBM)
anywhere = pl.BlockSpec(memory_space=pl.ANY)
mebi = 1024 * 1024


def call(name, kernel, held, far, passed, outs, scratch, work, limit, shared=None):
    operands = [
        *[pltpu.with_memory_space_constraint(value, pltpu.VMEM) for value in held],
        *[pltpu.with_memory_space_constraint(value, pltpu.HBM) for value in far],
    ]
    aliases = {len(operands) + n: len(outs) + n for n in range(len(passed))}
    if shared is not None:
        aliases[shared] = len(outs) - 1
    found = pl.pallas_call(
        functools.partial(kernel, len(held), len(far), len(passed), len(outs)),
        out_shape=list(outs) + [jax.ShapeDtypeStruct(value.shape, value.dtype) for value in passed],
        in_specs=[vmem] * len(held) + [hbm] * len(far) + [anywhere] * len(passed),
        out_specs=[vmem] * len(outs) + [anywhere] * len(passed),
        scratch_shapes=scratch,
        input_output_aliases=aliases,
        compiler_params=pltpu.CompilerParams(vmem_limit_bytes=limit * mebi),
        cost_estimate=pl.CostEstimate(flops=work * 1_000, bytes_accessed=100, transcendentals=0),
        name=name,
    )(*operands, *passed)
    return found[:len(outs)], found[len(outs):]


def sorted_refs(held, far, passed, outs, refs):
    after = held + far + passed
    return refs[:held], refs[held:held + far], refs[after:after + outs], refs[after + outs + passed:]


def placed():
    here = lax.axis_index("space")
    return here // 2, here % 2, lax.axis_index("tm")


def load_kernel(held, far, passed, outs, *refs):
    _, sources, targets, (ksp_buf, mask_buf, sems, small_sems) = sorted_refs(held, far, passed, outs, refs)
    tables = far - 7
    image, extrap, tv_dual, mask, coil, dual, kspace = sources[tables:]
    token, weight, image_out, here, pair, near, give = targets[tables:]
    token[...] = jnp.zeros(token.shape, token.dtype)
    copies = [
        pltpu.make_async_copy(mask, mask_buf, small_sems.at[tables]),
        pltpu.make_async_copy(image.at[:, 0], image_out, small_sems.at[tables + 1]),
        pltpu.make_async_copy(extrap.at[:, 0], here, small_sems.at[tables + 2]),
        pltpu.make_async_copy(extrap.at[:, 0], pair.at[0:2], small_sems.at[tables + 3]),
        pltpu.make_async_copy(tv_dual.at[:, 0], pair.at[2:4], small_sems.at[tables + 4]),
    ]
    copies += [pltpu.make_async_copy(sources[n], targets[n], small_sems.at[n]) for n in range(tables)]
    _, chips, _, height, _ = near.shape
    place = placed()
    loads = []
    for other, target in enumerate((near, give)):
        for offset in range(chips):
            plane = 2 * jnp.bitwise_xor(place[0], offset) + jnp.bitwise_xor(place[1], other)
            rows = pl.ds(pl.multiple_of(plane * height, height), height)
            loads.append([
                pltpu.make_async_copy(dual.at[:, 0, 0, plane], target.at[1, offset], sems.at[other, offset, 0]),
                pltpu.make_async_copy(kspace.at[:, 0, 0, plane], ksp_buf.at[other, offset], sems.at[other, offset, 1]),
                pltpu.make_async_copy(coil.at[:, 0, rows, :], target.at[0, offset], sems.at[other, offset, 2]),
            ])
    for load in loads:
        for copy in load:
            copy.start()
    for copy in copies:
        copy.start()
    for other, target in enumerate((near, give)):
        for offset in range(chips):
            for copy in loads[other * chips + offset]:
                copy.wait()
            for part in (0, 1):
                target[1, offset, part] = target[1, offset, part] - dual_step * ksp_buf[other, offset, part]
    for copy in copies:
        copy.wait()
    weight[...] = mask_buf[0].astype(jnp.float32) / (1.0 + dual_step)


def coil_kernel(first, held, far, passed, outs, *refs):
    values, _, targets, (u_buf, v_buf) = sorted_refs(held, far, passed, outs, refs)
    count = outs - 2
    blocks, sides = values[:count], values[count:count + 2]
    weight, col_fwd, even_fwd, odd_fwd, col_bwd, even_bwd, odd_bwd = values[count + 2:count + 9]
    totals, (new_own, new_all) = targets[:count], targets[count:]
    new_other = new_all.at[first:first + count]
    height, depth = weight.shape
    half = height // 2
    for n in range(count):

        def maps():
            return [(side[0, first + n, 0], side[0, first + n, 1]) for side in sides]

        image_re, image_im = blocks[n][0], blocks[n][1]
        real, imag = [], []
        for map_re, map_im in maps():
            real.append(map_re * image_re - map_im * image_im)
            imag.append(map_re * image_im + map_im * image_re)
        lines = columns_dft(jnp.concatenate(real, axis=0), jnp.concatenate(imag, axis=0), col_fwd[...])
        u_buf[0] = lines[:, :depth]
        u_buf[1] = lines[:, depth:]
        halves = []
        for odd, table in ((0, even_fwd), (1, odd_fwd)):
            cells = jnp.concatenate([
                jnp.concatenate([u_buf[part, pl.ds(c * height + odd, half, stride=2), :] for part in (0, 1)], axis=0)
                for c in (0, 1)
            ], axis=1)
            halves.append(rows_dft(table[...], cells))
        spectrum = (halves[0] + halves[1], halves[0] - halves[1])
        updated = []
        for q in (0, 1):
            span = pl.ds(q * half, half)
            columns = []
            for c, new in enumerate((new_own, new_other)):
                pieces = []
                for part in (0, 1):
                    value = spectrum[q][part * half:(part + 1) * half, c * depth:(c + 1) * depth]
                    piece = weight[span, :] * (sides[c][1, first + n, part, span, :] + dual_step * value)
                    new[n, part, span, :] = piece
                    pieces.append(piece)
                columns.append(jnp.concatenate(pieces, axis=0))
            updated.append(jnp.concatenate(columns, axis=1))
        for odd, table in ((0, even_bwd), (1, odd_bwd)):
            back = rows_dft(table[...], updated[0] - updated[1] if odd else updated[0] + updated[1])
            for c in (0, 1):
                for part in (0, 1):
                    v_buf[part, pl.ds(c * height + odd, half, stride=2), :] = back[
                        part * half:(part + 1) * half, c * depth:(c + 1) * depth
                    ]
        back = columns_dft(v_buf[0], v_buf[1], col_bwd[...])
        total_re, total_im = 0.0, 0.0
        for c, (map_re, map_im) in enumerate(maps()):
            back_re = back[c * height:(c + 1) * height, :depth]
            back_im = back[c * height:(c + 1) * height, depth:]
            total_re = total_re + map_re * back_re + map_im * back_im
            total_im = total_im + map_re * back_im - map_im * back_re
        totals[n][0] = total_re
        totals[n][1] = total_im


def project(moved):
    magnitude = jnp.sqrt(moved[0] * moved[0] + moved[1] * moved[1])
    factor = clip_level / jnp.maximum(magnitude, clip_level)
    return [value * factor for value in moved]


def temporal_kernel(total, held, far, passed, outs, *refs):
    (image, pair, pair_before, *others), _, (tv_new, begin), _ = sorted_refs(held, far, passed, outs, refs)
    current, dual = pair.at[0:2], pair.at[2:4]
    previous, dual_before = pair_before.at[0:2], pair_before.at[2:4]
    later = others[0] if others else previous
    place = placed()
    not_first = jnp.where(place[2] > 0, 1.0, 0.0)
    not_last = jnp.where(place[2] < total - 1, 1.0, 0.0)
    own = project([
        dual[part] + (dual_step * not_last) * (later[part] - current[part]) for part in (0, 1)
    ])
    earlier = project([
        dual_before[part] + dual_step * (current[part] - previous[part]) for part in (0, 1)
    ])
    for part in (0, 1):
        tv_new[part] = own[part]
        begin[part] = image[part] - primal_step * (not_first * earlier[part] - not_last * own[part])


def pass_kernel(held, far, passed, outs, *refs):
    pass


def sum_kernel(begun, held, far, passed, outs, *refs):
    values, _, (target,), _ = sorted_refs(held, far, passed, outs, refs)
    for part in (0, 1):
        total = 0.0
        for value in values[:held - begun]:
            total = total + value[part]
        target[part] = values[-1][part] - primal_step * total if begun else total


def store_kernel(*refs):
    groups, new_other, _, data_new, sems = refs[:-4], *refs[-4:]
    place = placed()
    count = groups[0].shape[0]
    stores = []
    for offset in range(new_other.shape[0]):
        for other, source in enumerate((groups[offset // count].at[offset % count], new_other.at[offset])):
            plane = 2 * jnp.bitwise_xor(place[0], offset) + jnp.bitwise_xor(place[1], other)
            stores.append(pltpu.make_async_copy(source, data_new.at[:, 0, 0, plane], sems.at[other, offset]))
            stores[-1].start()
    for store in stores:
        store.wait()


def turned(value, axis, steps):
    count = lax.axis_size(axis)
    return lax.ppermute(value, axis, [(source, (source + steps) % count) for source in range(count)])


def swapped(value, mask):
    count = lax.axis_size("space")
    return lax.ppermute(value, "space", [(source, source ^ mask) for source in range(count)])


def on_device(image, extrap, tv_dual, data_dual, kspace, coil_maps, sampling):
    height, depth = kspace.shape[4:]
    chips = lax.axis_size("space") // 2
    inner = chips // 4
    frame_total = lax.axis_size("tm")
    tables = [
        jnp.asarray(table)
        for table in (
            column_table(depth, -1), *row_tables(height, -1), column_table(depth, 1), *row_tables(height, 1)
        )
    ]
    block = pltpu.VMEM((2, height, depth), jnp.float32)
    result = jax.ShapeDtypeStruct((2, height, depth), jnp.float32)

    def ahead(work, token, *values):
        _, (token, *values) = call("ahead", pass_kernel, [], [], [token, *values], [], [], work, 2)
        return (token, *values)

    blocks = {i: swapped(extrap[:, 0], 2 * i) for i in range(1, inner + 1)}
    blocks[2 * inner] = swapped(extrap[:, 0], 4 * inner)

    half = pltpu.VMEM((2, chips, 2, height, depth), jnp.float32)
    (*tables, token, weight, image_here, blocks[0], pair, near, give), _ = call(
        "load", load_kernel, [], [*tables, image, extrap, tv_dual, sampling, coil_maps, data_dual, kspace], [],
        [pltpu.VMEM(value.shape, value.dtype) for value in tables]
        + [pltpu.VMEM((8, 128), jnp.float32), pltpu.VMEM((height, depth), jnp.float32)]
        + [block, block, pltpu.VMEM((4, height, depth), jnp.float32), half, half],
        [
            pltpu.VMEM((2, chips, 2, height, depth), jnp.float32),
            pltpu.VMEM((1, height, depth), jnp.int32),
            pltpu.SemaphoreType.DMA((2, chips, 3)),
            pltpu.SemaphoreType.DMA((len(tables) + 5,)),
        ],
        1, 4,
    )
    other = swapped(give, 1)
    pair_before = turned(pair, "tm", 1)
    later = [] if frame_total == 2 else [turned(blocks[0], "tm", -1)]

    totals, new_own = {}, {}

    def coils(z, token, new_other):
        held = [blocks[z * inner + i] for i in range(inner)] + [near, other, weight, *tables]
        found, (token,) = call(
            "coils", functools.partial(coil_kernel, z * inner), held + new_other, [], [token],
            [block] * inner + [
                pltpu.VMEM((inner, 2, height, depth), jnp.float32), pltpu.VMEM((chips, 2, height, depth), jnp.float32)
            ],
            [pltpu.VMEM((2, 2 * height, depth), jnp.float32)] * 2,
            100_000, 8, len(held) if new_other else None,
        )
        totals[z], new_own[z] = found[:inner], found[inner]
        arrived[z] = [swapped(totals[z][i], 2 * i) for i in range(1, inner)]
        return token, [found[inner + 1]]

    def onward(z, token):
        (found,), (token,) = call(
            "sums", functools.partial(sum_kernel, 0), [totals[z][0], *arrived[z]], [], [token], [block], [],
            50, 2,
        )
        return found, token

    arrived, parts = {}, {}
    token, *found = ahead(30_000_000, token, *[blocks[i] for i in range(1, inner + 1)], blocks[2 * inner])
    blocks.update(zip([*range(1, inner + 1), 2 * inner], found))
    blocks[3 * inner] = swapped(blocks[2 * inner], 2 * inner)
    for z in (1, 2):
        for i in range(1, inner):
            blocks[z * inner + i] = swapped(blocks[z * inner], 2 * i)
    token, new_other = coils(0, token, [])
    token, blocks[3 * inner] = ahead(1, token, blocks[3 * inner])
    for i in range(1, inner):
        blocks[3 * inner + i] = swapped(blocks[3 * inner], 2 * i)
    for z in (2, 1, 3):
        token, new_other = coils(z, token, new_other)
    parts[2], token = onward(2, token)
    (tv_here, begin), (token,) = call(
        "temporal", functools.partial(temporal_kernel, frame_total), [image_here, pair, pair_before, *later], [], [token],
        [result, block], [], 50, 4,
    )
    for z in (1, 3):
        parts[z], token = onward(z, token)
    parts = [swapped(parts[z], 2 * z * inner) for z in (1, 2, 3)]
    new_other = swapped(new_other[0], 1)
    (begin,), (token,) = call(
        "sums", functools.partial(sum_kernel, 1), [totals[0][0], *parts[:2], begin], [], [token], [block], [],
        20_000_000, 2,
    )
    (image_new,), _ = call(
        "sums", functools.partial(sum_kernel, 1), [*arrived[0], parts[2], begin], [], [], [result], [], 1, 2,
    )

    groups = [new_own[z] for z in range(4)] + [new_other, token]
    data_new = pl.pallas_call(
        store_kernel,
        out_shape=jax.ShapeDtypeStruct(kspace.shape, jnp.float32),
        in_specs=[vmem] * len(groups),
        out_specs=hbm,
        scratch_shapes=[pltpu.SemaphoreType.DMA((2, chips))],
        compiler_params=pltpu.CompilerParams(vmem_limit_bytes=2 * mebi),
        cost_estimate=pl.CostEstimate(flops=1_000, bytes_accessed=100, transcendentals=0),
        name="store",
    )(*groups)
    return (image_new[:, None], tv_here[:, None], data_new)


def passed_along(value, axis, steps):
    count = lax.axis_size(axis)
    initial, last = (max(0, -steps), min(count, count - steps))
    return lax.ppermute(value, axis, [(source, source + steps) for source in range(initial, last)])


def plain_tables(length):
    places = lax.iota(jnp.int32, length)
    product = places[:, None] * places[None, :] % length
    angles = product.astype(jnp.float32) * (2.0 * math.pi / length)
    factor = 1.0 / math.sqrt(length)
    return (jnp.cos(angles) * factor, jnp.sin(angles) * factor)


def right_mult(values, table):
    return jnp.dot(values, table, precision=lax.Precision.HIGHEST, preferred_element_type=jnp.float32)


def left_mult(table, values):
    return jnp.einsum(
        "ky,cxyz->cxkz", table, values, precision=lax.Precision.HIGHEST, preferred_element_type=jnp.float32
    )


def on_any(image, extrap, tv_dual, data_dual, kspace, coil_maps, sampling):
    readout = kspace.shape[3]
    height = kspace.shape[4]
    depth = kspace.shape[5]
    coil_count = kspace.shape[2]
    own_rows = image.shape[2]
    cos_cols, sin_cols = plain_tables(depth)
    cos_rows, sin_rows = plain_tables(height)
    frame_here = lax.axis_index("tm")
    frame_total = lax.axis_size("tm")
    not_last = (frame_here < frame_total - 1).astype(jnp.float32)
    current = extrap[:, 0]
    later = passed_along(current, "tm", -1)
    moved = tv_dual[:, 0] + dual_step * not_last * (later - current)
    tv_real, tv_imag = project(moved)
    tv_here = jnp.stack([tv_real, tv_imag])
    piece = lax.all_gather(current, "space", axis=1, tiled=True)
    piece_real = piece[0][None]
    piece_imag = piece[1][None]
    coil_real = coil_maps[0] * piece_real - coil_maps[1] * piece_imag
    coil_imag = coil_maps[0] * piece_imag + coil_maps[1] * piece_real
    out_real = right_mult(coil_real, cos_cols) + right_mult(coil_imag, sin_cols)
    out_imag = right_mult(coil_imag, cos_cols) - right_mult(coil_real, sin_cols)
    half_spectrum = jnp.stack([out_real, out_imag])
    half_spectrum = half_spectrum.reshape(2, coil_count, readout, height, depth)
    spec_real = left_mult(cos_rows, half_spectrum[0]) + left_mult(sin_rows, half_spectrum[1])
    spec_imag = left_mult(cos_rows, half_spectrum[1]) - left_mult(sin_rows, half_spectrum[0])
    weight = sampling[0].astype(jnp.float32)
    scaled = weight / (1.0 + dual_step)
    dual_real = scaled * (data_dual[0, 0] + dual_step * (spec_real - kspace[0, 0]))
    dual_imag = scaled * (data_dual[1, 0] + dual_step * (spec_imag - kspace[1, 0]))
    back_real = left_mult(cos_rows, dual_real) - left_mult(sin_rows, dual_imag)
    back_imag = left_mult(cos_rows, dual_imag) + left_mult(sin_rows, dual_real)
    back_real = back_real.reshape(coil_count, readout * height, depth)
    back_imag = back_imag.reshape(coil_count, readout * height, depth)
    plane_real = right_mult(back_real, cos_cols) - right_mult(back_imag, sin_cols)
    plane_imag = right_mult(back_imag, cos_cols) + right_mult(back_real, sin_cols)
    term_real = jnp.sum(coil_maps[0] * plane_real + coil_maps[1] * plane_imag, axis=0)
    term_imag = jnp.sum(coil_maps[0] * plane_imag - coil_maps[1] * plane_real, axis=0)
    coil_term = jnp.stack([term_real, term_imag])
    combined = lax.psum(coil_term, "space")
    adjoint = lax.dynamic_slice_in_dim(combined, lax.axis_index("space") * own_rows, own_rows, 1)
    earlier = passed_along(tv_here, "tm", 1)
    temporal = earlier - not_last * tv_here
    image_new = image[:, 0] - primal_step * (adjoint + temporal)
    data_new = jnp.stack([dual_real, dual_imag])[:, None]
    return (image_new[:, None], tv_here[:, None], data_new)


def solution(mesh):
    in_specs = (
        P(None, "tm", "space", None),
        P(None, "tm", "space", None),
        P(None, "tm", "space", None),
        P(None, "tm", "space", None, None, None),
        P(None, "tm", "space", None, None, None),
        P(None, "space", None, None),
        P("tm", None, None),
    )
    out_specs = (
        P(None, "tm", "space", None),
        P(None, "tm", "space", None),
        P(None, "tm", "space", None, None, None),
    )

    def either(*local):
        kspace = local[4]
        one_plane = local[0].shape[2] == kspace.shape[4] and mesh.shape["space"] == kspace.shape[3]
        paired = mesh.shape["space"] % 8 == 0 and mesh.shape["space"] & (mesh.shape["space"] - 1) == 0
        return (on_device if one_plane and paired else on_any)(*local)

    return jax.shard_map(
        either, mesh=mesh, in_specs=in_specs, out_specs=out_specs, check_vma=False
    )
```

```python
import functools
import math

import jax
import jax.numpy as jnp
import ml_dtypes
import numpy as np
from jax import lax
from jax.experimental import pallas as pl
from jax.experimental.pallas import tpu as pltpu
from jax.sharding import PartitionSpec as P

dual_step = 0.4
primal_step = 0.4
clip_level = 0.5


def split_host(table):
    high = table.astype(ml_dtypes.bfloat16)
    low = (table - high.astype(np.float64)).astype(ml_dtypes.bfloat16)
    return high, low


def column_table(length, sign):
    places = np.arange(length)
    angles = 2.0 * math.pi * (np.outer(places, places) % length) / length
    real = np.cos(angles) / math.sqrt(length)
    imag = sign * np.sin(angles) / math.sqrt(length)
    whole = np.block([[real, imag], [-imag, real]])
    high, low = split_host(whole)
    return np.concatenate([high, high, low], axis=0)


def row_tables(length, sign):
    half = length // 2
    found = []
    for odd in (0, 1):
        lines = np.arange(half)
        cells = 2 * np.arange(half) + odd
        product = np.outer(lines, cells)
        angles = 2.0 * math.pi * (product % length) / length
        real = np.cos(angles) / math.sqrt(length)
        imag = sign * np.sin(angles) / math.sqrt(length)
        if sign > 0:
            real, imag = real.T, imag.T
        whole = np.block([[real, -imag], [imag, real]])
        high, low = split_host(whole)
        found.append(np.concatenate([high, high, low], axis=1))
    return found


def split(values):
    high = values.astype(jnp.bfloat16)
    low = (values - high.astype(jnp.float32)).astype(jnp.bfloat16)
    return high, low


def columns_dft(real, imag, table):
    real_high, real_low = split(real)
    imag_high, imag_low = split(imag)
    left = jnp.concatenate([real_high, imag_high, real_low, imag_low, real_high, imag_high], axis=1)
    return jnp.dot(left, table, preferred_element_type=jnp.float32)


def rows_dft(table, values):
    high, low = split(values)
    return jnp.dot(table, jnp.concatenate([high, low, high], axis=0), preferred_element_type=jnp.float32)


vmem = pl.BlockSpec(memory_space=pltpu.VMEM)
hbm = pl.BlockSpec(memory_space=pltpu.HBM)
anywhere = pl.BlockSpec(memory_space=pl.ANY)
mebi = 1024 * 1024


def call(name, kernel, held, far, passed, outs, scratch, work, limit, shared=None):
    operands = [
        *[pltpu.with_memory_space_constraint(value, pltpu.VMEM) for value in held],
        *[pltpu.with_memory_space_constraint(value, pltpu.HBM) for value in far],
    ]
    aliases = {len(operands) + n: len(outs) + n for n in range(len(passed))}
    if shared is not None:
        aliases[shared] = len(outs) - 1
    found = pl.pallas_call(
        functools.partial(kernel, len(held), len(far), len(passed), len(outs)),
        out_shape=list(outs) + [jax.ShapeDtypeStruct(value.shape, value.dtype) for value in passed],
        in_specs=[vmem] * len(held) + [hbm] * len(far) + [anywhere] * len(passed),
        out_specs=[vmem] * len(outs) + [anywhere] * len(passed),
        scratch_shapes=scratch,
        input_output_aliases=aliases,
        compiler_params=pltpu.CompilerParams(vmem_limit_bytes=limit * mebi),
        cost_estimate=pl.CostEstimate(flops=work * 1_000, bytes_accessed=100, transcendentals=0),
        name=name,
    )(*operands, *passed)
    return found[:len(outs)], found[len(outs):]


def sorted_refs(held, far, passed, outs, refs):
    after = held + far + passed
    return refs[:held], refs[held:held + far], refs[after:after + outs], refs[after + outs + passed:]


def placed():
    here = lax.axis_index("space")
    return here // 2, here % 2, lax.axis_index("tm")


def load_kernel(held, far, passed, outs, *refs):
    _, sources, targets, (ksp_buf, mask_buf, sems, small_sems) = sorted_refs(held, far, passed, outs, refs)
    tables = far - 7
    image, extrap, tv_dual, mask, coil, dual, kspace = sources[tables:]
    token, weight, image_out, here, pair, near, give = targets[tables:]
    token[...] = jnp.zeros(token.shape, token.dtype)
    copies = [
        pltpu.make_async_copy(mask, mask_buf, small_sems.at[tables]),
        pltpu.make_async_copy(image.at[:, 0], image_out, small_sems.at[tables + 1]),
        pltpu.make_async_copy(extrap.at[:, 0], here, small_sems.at[tables + 2]),
        pltpu.make_async_copy(extrap.at[:, 0], pair.at[0:2], small_sems.at[tables + 3]),
        pltpu.make_async_copy(tv_dual.at[:, 0], pair.at[2:4], small_sems.at[tables + 4]),
    ]
    copies += [pltpu.make_async_copy(sources[n], targets[n], small_sems.at[n]) for n in range(tables)]
    _, chips, _, height, _ = near.shape
    place = placed()
    loads = []
    for other, target in enumerate((near, give)):
        for offset in range(chips):
            plane = 2 * jnp.bitwise_xor(place[0], offset) + jnp.bitwise_xor(place[1], other)
            rows = pl.ds(pl.multiple_of(plane * height, height), height)
            loads.append([
                pltpu.make_async_copy(dual.at[:, 0, 0, plane], target.at[1, offset], sems.at[other, offset, 0]),
                pltpu.make_async_copy(kspace.at[:, 0, 0, plane], ksp_buf.at[other, offset], sems.at[other, offset, 1]),
                pltpu.make_async_copy(coil.at[:, 0, rows, :], target.at[0, offset], sems.at[other, offset, 2]),
            ])
    for load in loads:
        for copy in load:
            copy.start()
    for copy in copies:
        copy.start()
    for other, target in enumerate((near, give)):
        for offset in range(chips):
            for copy in loads[other * chips + offset]:
                copy.wait()
            for part in (0, 1):
                target[1, offset, part] = target[1, offset, part] - dual_step * ksp_buf[other, offset, part]
    for copy in copies:
        copy.wait()
    weight[...] = mask_buf[0].astype(jnp.float32) / (1.0 + dual_step)


def coil_kernel(first, count, held, far, passed, outs, *refs):
    values, _, targets, (u_buf, v_buf) = sorted_refs(held, far, passed, outs, refs)
    sides = values[:2]
    weight, col_fwd, even_fwd, odd_fwd, col_bwd, even_bwd, odd_bwd = values[2:9]
    blocks = values[9:9 + count] if values[9].ndim == 3 else [values[9].at[n] for n in range(count)]
    totals, (new_own, *packed, new_all) = targets[:count], targets[count:]
    if packed:
        for n in range(count):
            packed[0][n] = blocks[n][...]
    new_other = new_all.at[first:first + count]
    height, depth = weight.shape
    half = height // 2
    for n in range(count):

        def maps():
            return [(side[0, first + n, 0], side[0, first + n, 1]) for side in sides]

        image_re, image_im = blocks[n][0], blocks[n][1]
        real, imag = [], []
        for map_re, map_im in maps():
            real.append(map_re * image_re - map_im * image_im)
            imag.append(map_re * image_im + map_im * image_re)
        lines = columns_dft(jnp.concatenate(real, axis=0), jnp.concatenate(imag, axis=0), col_fwd[...])
        u_buf[0] = lines[:, :depth]
        u_buf[1] = lines[:, depth:]
        halves = []
        for odd, table in ((0, even_fwd), (1, odd_fwd)):
            cells = jnp.concatenate([
                jnp.concatenate([u_buf[part, pl.ds(c * height + odd, half, stride=2), :] for part in (0, 1)], axis=0)
                for c in (0, 1)
            ], axis=1)
            halves.append(rows_dft(table[...], cells))
        spectrum = (halves[0] + halves[1], halves[0] - halves[1])
        updated = []
        for q in (0, 1):
            span = pl.ds(q * half, half)
            columns = []
            for c, new in enumerate((new_own, new_other)):
                pieces = []
                for part in (0, 1):
                    value = spectrum[q][part * half:(part + 1) * half, c * depth:(c + 1) * depth]
                    piece = weight[span, :] * (sides[c][1, first + n, part, span, :] + dual_step * value)
                    new[n, part, span, :] = piece
                    pieces.append(piece)
                columns.append(jnp.concatenate(pieces, axis=0))
            updated.append(jnp.concatenate(columns, axis=1))
        for odd, table in ((0, even_bwd), (1, odd_bwd)):
            back = rows_dft(table[...], updated[0] - updated[1] if odd else updated[0] + updated[1])
            for c in (0, 1):
                for part in (0, 1):
                    v_buf[part, pl.ds(c * height + odd, half, stride=2), :] = back[
                        part * half:(part + 1) * half, c * depth:(c + 1) * depth
                    ]
        back = columns_dft(v_buf[0], v_buf[1], col_bwd[...])
        total_re, total_im = 0.0, 0.0
        for c, (map_re, map_im) in enumerate(maps()):
            back_re = back[c * height:(c + 1) * height, :depth]
            back_im = back[c * height:(c + 1) * height, depth:]
            total_re = total_re + map_re * back_re + map_im * back_im
            total_im = total_im + map_re * back_im - map_im * back_re
        totals[n][0] = total_re
        totals[n][1] = total_im


def project(moved):
    magnitude = jnp.sqrt(moved[0] * moved[0] + moved[1] * moved[1])
    factor = clip_level / jnp.maximum(magnitude, clip_level)
    return [value * factor for value in moved]


def temporal_kernel(total, held, far, passed, outs, *refs):
    (image, pair, pair_before, *others), _, (tv_new, begin), _ = sorted_refs(held, far, passed, outs, refs)
    current, dual = pair.at[0:2], pair.at[2:4]
    previous, dual_before = pair_before.at[0:2], pair_before.at[2:4]
    later = others[0] if others else previous
    place = placed()
    not_first = jnp.where(place[2] > 0, 1.0, 0.0)
    not_last = jnp.where(place[2] < total - 1, 1.0, 0.0)
    own = project([
        dual[part] + (dual_step * not_last) * (later[part] - current[part]) for part in (0, 1)
    ])
    earlier = project([
        dual_before[part] + dual_step * (current[part] - previous[part]) for part in (0, 1)
    ])
    for part in (0, 1):
        tv_new[part] = own[part]
        begin[part] = image[part] - primal_step * (not_first * earlier[part] - not_last * own[part])


def pass_kernel(held, far, passed, outs, *refs):
    pass


def sum_kernel(begun, held, far, passed, outs, *refs):
    values, _, (target,), _ = sorted_refs(held, far, passed, outs, refs)
    for part in (0, 1):
        total = 0.0
        for value in values[:held - begun]:
            total = total + value[part]
        target[part] = values[-1][part] - primal_step * total if begun else total


def store_kernel(other, count, *refs):
    groups, data_new, sems = refs[:count], refs[-3], refs[-1]
    place = placed()
    stores = []
    for g, group in enumerate(groups):
        for n in range(group.shape[0]):
            offset = g * group.shape[0] + n
            plane = 2 * jnp.bitwise_xor(place[0], offset) + jnp.bitwise_xor(place[1], other)
            stores.append(pltpu.make_async_copy(group.at[n], data_new.at[:, 0, 0, plane], sems.at[offset]))
            stores[-1].start()
    for store in stores:
        store.wait()


def turned(value, axis, steps):
    count = lax.axis_size(axis)
    return lax.ppermute(value, axis, [(source, (source + steps) % count) for source in range(count)])


def swapped(value, mask):
    count = lax.axis_size("space")
    return lax.ppermute(value, "space", [(source, source ^ mask) for source in range(count)])


def on_device(image, extrap, tv_dual, data_dual, kspace, coil_maps, sampling):
    height, depth = kspace.shape[4:]
    chips = lax.axis_size("space") // 2
    inner = chips // 4
    frame_total = lax.axis_size("tm")
    tables = [
        jnp.asarray(table)
        for table in (
            column_table(depth, -1), *row_tables(height, -1), column_table(depth, 1), *row_tables(height, 1)
        )
    ]
    block = pltpu.VMEM((2, height, depth), jnp.float32)
    result = jax.ShapeDtypeStruct((2, height, depth), jnp.float32)

    def ahead(work, token, *values):
        _, (token, *values) = call("ahead", pass_kernel, [], [], [token, *values], [], [], work, 2)
        return (token, *values)

    blocks = {2 * inner: swapped(extrap[:, 0], 4 * inner)}
    for i in range(1, inner):
        blocks[i] = swapped(extrap[:, 0], 2 * i)

    half = pltpu.VMEM((2, chips, 2, height, depth), jnp.float32)
    (*tables, token, weight, image_here, blocks[0], pair, near, give), _ = call(
        "load", load_kernel, [], [*tables, image, extrap, tv_dual, sampling, coil_maps, data_dual, kspace], [],
        [pltpu.VMEM(value.shape, value.dtype) for value in tables]
        + [pltpu.VMEM((8, 128), jnp.float32), pltpu.VMEM((height, depth), jnp.float32)]
        + [block, block, pltpu.VMEM((4, height, depth), jnp.float32), half, half],
        [
            pltpu.VMEM((2, chips, 2, height, depth), jnp.float32),
            pltpu.VMEM((1, height, depth), jnp.int32),
            pltpu.SemaphoreType.DMA((2, chips, 3)),
            pltpu.SemaphoreType.DMA((len(tables) + 5,)),
        ],
        1, 4,
    )
    other = swapped(give, 1)
    pair_before = turned(pair, "tm", 1)
    later = [] if frame_total == 2 else [turned(blocks[0], "tm", -1)]

    def store(name, whose, groups, before, token):
        operands = [pltpu.with_memory_space_constraint(value, pltpu.VMEM) for value in groups]
        operands += [pltpu.with_memory_space_constraint(value, pltpu.HBM) for value in before] + [token]
        return pl.pallas_call(
            functools.partial(store_kernel, whose, len(groups)),
            out_shape=[
                jax.ShapeDtypeStruct(kspace.shape, jnp.float32), jax.ShapeDtypeStruct(token.shape, token.dtype)
            ],
            in_specs=[vmem] * len(groups) + [hbm] * len(before) + [anywhere],
            out_specs=[hbm, anywhere],
            scratch_shapes=[pltpu.SemaphoreType.DMA((chips,))],
            input_output_aliases={len(groups) + n: n for n in (range(2) if before else ())} or {len(groups): 1},
            compiler_params=pltpu.CompilerParams(vmem_limit_bytes=2 * mebi),
            cost_estimate=pl.CostEstimate(flops=1_000, bytes_accessed=100, transcendentals=0),
            name=name,
        )(*operands)

    totals, new_own = {}, {}

    def coils(z, token, arrays, new_other, packs=False):
        held = [near, other, weight, *tables, *arrays, *new_other]
        found, (token,) = call(
            "coils", functools.partial(coil_kernel, z * inner, inner), held, [], [token],
            [block] * inner + [pltpu.VMEM((inner, 2, height, depth), jnp.float32)] * (2 if packs else 1)
            + [pltpu.VMEM((chips, 2, height, depth), jnp.float32)],
            [pltpu.VMEM((2, 2 * height, depth), jnp.float32)] * 2,
            100_000, 8, len(held) - 1 if new_other else None,
        )
        totals[z], new_own[z] = list(found[:inner]), found[inner]
        return (token, found[-1:], *(found[inner + 1:-1]))

    def beside(z):
        return [swapped(totals[z][i], 2 * i) for i in range(1, inner)]

    def sums(values, passed, work):
        (found,), passed = call("sums", functools.partial(sum_kernel, 0), values, [], passed, [block], [], work, 2)
        return (found, *passed)

    token, blocks[2 * inner] = ahead(30_000_000, token, blocks[2 * inner])
    for i in range(inner):
        blocks[3 * inner + i] = swapped(blocks[2 * inner], 2 * (inner + i))
    for i in range(1, inner):
        blocks[2 * inner + i] = swapped(blocks[2 * inner], 2 * i)
    token, new_other, pack = coils(0, token, [blocks[i] for i in range(inner)], [], True)
    pack = swapped(pack, 2 * inner)
    for z in (2, 3):
        token, new_other = coils(z, token, [blocks[z * inner + i] for i in range(inner)], new_other)
    beside_far = beside(3)
    part, token = sums([totals[2][0], *beside(2)], [token], 1_900_000)
    from_2 = swapped(part, 4 * inner)
    token, new_other = coils(1, token, [pack], new_other)
    part, token, *totals[1][1:] = sums([totals[3][0], *beside_far], [token, *totals[1][1:]], 50)
    from_3 = swapped(part, 6 * inner)
    total, token, *totals[0][1:] = sums([totals[0][0], from_2], [token, *totals[0][1:]], 300_000)
    part, token = sums([totals[1][0], *beside(1)], [token], 50)
    from_1 = swapped(part, 2 * inner)
    (tv_here, begin), (token,) = call(
        "temporal", functools.partial(temporal_kernel, frame_total), [image_here, pair, pair_before, *later], [], [token],
        [result, block], [], 50, 4,
    )
    data_new, token = store("store", 0, [new_own[z] for z in range(4)], [], token)
    total, token = sums([total, from_3], [token], 50_000)
    (image_new,), (token,) = call(
        "sums", functools.partial(sum_kernel, 1), [total, from_1, *beside(0), begin], [], [token], [result], [],
        20_000_000, 2,
    )
    data_new, _ = store("store", 1, [swapped(new_other[0], 1)], [data_new], token)
    return (image_new[:, None], tv_here[:, None], data_new)


def passed_along(value, axis, steps):
    count = lax.axis_size(axis)
    initial, last = (max(0, -steps), min(count, count - steps))
    return lax.ppermute(value, axis, [(source, source + steps) for source in range(initial, last)])


def plain_tables(length):
    places = lax.iota(jnp.int32, length)
    product = places[:, None] * places[None, :] % length
    angles = product.astype(jnp.float32) * (2.0 * math.pi / length)
    factor = 1.0 / math.sqrt(length)
    return (jnp.cos(angles) * factor, jnp.sin(angles) * factor)


def right_mult(values, table):
    return jnp.dot(values, table, precision=lax.Precision.HIGHEST, preferred_element_type=jnp.float32)


def left_mult(table, values):
    return jnp.einsum(
        "ky,cxyz->cxkz", table, values, precision=lax.Precision.HIGHEST, preferred_element_type=jnp.float32
    )


def on_any(image, extrap, tv_dual, data_dual, kspace, coil_maps, sampling):
    readout = kspace.shape[3]
    height = kspace.shape[4]
    depth = kspace.shape[5]
    coil_count = kspace.shape[2]
    own_rows = image.shape[2]
    cos_cols, sin_cols = plain_tables(depth)
    cos_rows, sin_rows = plain_tables(height)
    frame_here = lax.axis_index("tm")
    frame_total = lax.axis_size("tm")
    not_last = (frame_here < frame_total - 1).astype(jnp.float32)
    current = extrap[:, 0]
    later = passed_along(current, "tm", -1)
    moved = tv_dual[:, 0] + dual_step * not_last * (later - current)
    tv_real, tv_imag = project(moved)
    tv_here = jnp.stack([tv_real, tv_imag])
    piece = lax.all_gather(current, "space", axis=1, tiled=True)
    piece_real = piece[0][None]
    piece_imag = piece[1][None]
    coil_real = coil_maps[0] * piece_real - coil_maps[1] * piece_imag
    coil_imag = coil_maps[0] * piece_imag + coil_maps[1] * piece_real
    out_real = right_mult(coil_real, cos_cols) + right_mult(coil_imag, sin_cols)
    out_imag = right_mult(coil_imag, cos_cols) - right_mult(coil_real, sin_cols)
    half_spectrum = jnp.stack([out_real, out_imag])
    half_spectrum = half_spectrum.reshape(2, coil_count, readout, height, depth)
    spec_real = left_mult(cos_rows, half_spectrum[0]) + left_mult(sin_rows, half_spectrum[1])
    spec_imag = left_mult(cos_rows, half_spectrum[1]) - left_mult(sin_rows, half_spectrum[0])
    weight = sampling[0].astype(jnp.float32)
    scaled = weight / (1.0 + dual_step)
    dual_real = scaled * (data_dual[0, 0] + dual_step * (spec_real - kspace[0, 0]))
    dual_imag = scaled * (data_dual[1, 0] + dual_step * (spec_imag - kspace[1, 0]))
    back_real = left_mult(cos_rows, dual_real) - left_mult(sin_rows, dual_imag)
    back_imag = left_mult(cos_rows, dual_imag) + left_mult(sin_rows, dual_real)
    back_real = back_real.reshape(coil_count, readout * height, depth)
    back_imag = back_imag.reshape(coil_count, readout * height, depth)
    plane_real = right_mult(back_real, cos_cols) - right_mult(back_imag, sin_cols)
    plane_imag = right_mult(back_imag, cos_cols) + right_mult(back_real, sin_cols)
    term_real = jnp.sum(coil_maps[0] * plane_real + coil_maps[1] * plane_imag, axis=0)
    term_imag = jnp.sum(coil_maps[0] * plane_imag - coil_maps[1] * plane_real, axis=0)
    coil_term = jnp.stack([term_real, term_imag])
    combined = lax.psum(coil_term, "space")
    adjoint = lax.dynamic_slice_in_dim(combined, lax.axis_index("space") * own_rows, own_rows, 1)
    earlier = passed_along(tv_here, "tm", 1)
    temporal = earlier - not_last * tv_here
    image_new = image[:, 0] - primal_step * (adjoint + temporal)
    data_new = jnp.stack([dual_real, dual_imag])[:, None]
    return (image_new[:, None], tv_here[:, None], data_new)


def solution(mesh):
    in_specs = (
        P(None, "tm", "space", None),
        P(None, "tm", "space", None),
        P(None, "tm", "space", None),
        P(None, "tm", "space", None, None, None),
        P(None, "tm", "space", None, None, None),
        P(None, "space", None, None),
        P("tm", None, None),
    )
    out_specs = (
        P(None, "tm", "space", None),
        P(None, "tm", "space", None),
        P(None, "tm", "space", None, None, None),
    )

    def either(*local):
        kspace = local[4]
        one_plane = local[0].shape[2] == kspace.shape[4] and mesh.shape["space"] == kspace.shape[3]
        paired = mesh.shape["space"] % 8 == 0 and mesh.shape["space"] & (mesh.shape["space"] - 1) == 0
        return (on_device if one_plane and paired else on_any)(*local)

    return jax.shard_map(
        either, mesh=mesh, in_specs=in_specs, out_specs=out_specs, check_vma=False
    )
```

```python
import functools
import math

import jax
import jax.numpy as jnp
import ml_dtypes
import numpy as np
from jax import lax
from jax.experimental import pallas as pl
from jax.experimental.pallas import tpu as pltpu
from jax.sharding import PartitionSpec as P

dual_step = 0.4
primal_step = 0.4
clip_level = 0.5


def split_host(table):
    high = table.astype(ml_dtypes.bfloat16)
    low = (table - high.astype(np.float64)).astype(ml_dtypes.bfloat16)
    return high, low


def column_table(length, sign):
    places = np.arange(length)
    angles = 2.0 * math.pi * (np.outer(places, places) % length) / length
    real = np.cos(angles) / math.sqrt(length)
    imag = sign * np.sin(angles) / math.sqrt(length)
    whole = np.block([[real, imag], [-imag, real]])
    high, low = split_host(whole)
    return np.concatenate([high, high, low], axis=0)


def row_tables(length, sign):
    half = length // 2
    found = []
    for odd in (0, 1):
        lines = np.arange(half)
        cells = 2 * np.arange(half) + odd
        product = np.outer(lines, cells)
        angles = 2.0 * math.pi * (product % length) / length
        real = np.cos(angles) / math.sqrt(length)
        imag = sign * np.sin(angles) / math.sqrt(length)
        if sign > 0:
            real, imag = real.T, imag.T
        whole = np.block([[real, -imag], [imag, real]])
        high, low = split_host(whole)
        found.append(np.concatenate([high, high, low], axis=1))
    return found


def split(values):
    high = values.astype(jnp.bfloat16)
    low = (values - high.astype(jnp.float32)).astype(jnp.bfloat16)
    return high, low


def columns_dft(real, imag, table):
    real_high, real_low = split(real)
    imag_high, imag_low = split(imag)
    left = jnp.concatenate([real_high, imag_high, real_low, imag_low, real_high, imag_high], axis=1)
    return jnp.dot(left, table, preferred_element_type=jnp.float32)


def rows_dft(table, values):
    high, low = split(values)
    return jnp.dot(table, jnp.concatenate([high, low, high], axis=0), preferred_element_type=jnp.float32)


vmem = pl.BlockSpec(memory_space=pltpu.VMEM)
hbm = pl.BlockSpec(memory_space=pltpu.HBM)
anywhere = pl.BlockSpec(memory_space=pl.ANY)
mebi = 1024 * 1024


def call(name, kernel, held, far, passed, outs, scratch, work, limit, shared=None):
    operands = [
        *[pltpu.with_memory_space_constraint(value, pltpu.VMEM) for value in held],
        *[pltpu.with_memory_space_constraint(value, pltpu.HBM) for value in far],
    ]
    aliases = {len(operands) + n: len(outs) + n for n in range(len(passed))}
    if shared is not None:
        aliases[shared] = len(outs) - 1
    found = pl.pallas_call(
        functools.partial(kernel, len(held), len(far), len(passed), len(outs)),
        out_shape=list(outs) + [jax.ShapeDtypeStruct(value.shape, value.dtype) for value in passed],
        in_specs=[vmem] * len(held) + [hbm] * len(far) + [anywhere] * len(passed),
        out_specs=[vmem] * len(outs) + [anywhere] * len(passed),
        scratch_shapes=scratch,
        input_output_aliases=aliases,
        compiler_params=pltpu.CompilerParams(vmem_limit_bytes=limit * mebi),
        cost_estimate=pl.CostEstimate(flops=work * 1_000, bytes_accessed=100, transcendentals=0),
        name=name,
    )(*operands, *passed)
    return found[:len(outs)], found[len(outs):]


def sorted_refs(held, far, passed, outs, refs):
    after = held + far + passed
    return refs[:held], refs[held:held + far], refs[after:after + outs], refs[after + outs + passed:]


def placed():
    here = lax.axis_index("space")
    return here // 2, here % 2, lax.axis_index("tm")


def load_kernel(held, far, passed, outs, *refs):
    _, sources, targets, (ksp_buf, mask_buf, sems, small_sems) = sorted_refs(held, far, passed, outs, refs)
    tables = far - 7
    image, extrap, tv_dual, mask, coil, dual, kspace = sources[tables:]
    token, weight, image_out, here, pair, near, give = targets[tables:]
    token[...] = jnp.zeros(token.shape, token.dtype)
    copies = [
        pltpu.make_async_copy(mask, mask_buf, small_sems.at[tables]),
        pltpu.make_async_copy(image.at[:, 0], image_out, small_sems.at[tables + 1]),
        pltpu.make_async_copy(extrap.at[:, 0], here, small_sems.at[tables + 2]),
        pltpu.make_async_copy(extrap.at[:, 0], pair.at[0:2], small_sems.at[tables + 3]),
        pltpu.make_async_copy(tv_dual.at[:, 0], pair.at[2:4], small_sems.at[tables + 4]),
    ]
    copies += [pltpu.make_async_copy(sources[n], targets[n], small_sems.at[n]) for n in range(tables)]
    _, chips, _, height, _ = near.shape
    place = placed()
    loads = []
    for other, target in enumerate((near, give)):
        for offset in range(chips):
            plane = 2 * jnp.bitwise_xor(place[0], offset) + jnp.bitwise_xor(place[1], other)
            rows = pl.ds(pl.multiple_of(plane * height, height), height)
            loads.append([
                pltpu.make_async_copy(dual.at[:, 0, 0, plane], target.at[1, offset], sems.at[other, offset, 0]),
                pltpu.make_async_copy(kspace.at[:, 0, 0, plane], ksp_buf.at[other, offset], sems.at[other, offset, 1]),
                pltpu.make_async_copy(coil.at[:, 0, rows, :], target.at[0, offset], sems.at[other, offset, 2]),
            ])
    for load in loads:
        for copy in load:
            copy.start()
    for copy in copies:
        copy.start()
    for other, target in enumerate((near, give)):
        for offset in range(chips):
            for copy in loads[other * chips + offset]:
                copy.wait()
            for part in (0, 1):
                target[1, offset, part] = target[1, offset, part] - dual_step * ksp_buf[other, offset, part]
    for copy in copies:
        copy.wait()
    weight[...] = mask_buf[0].astype(jnp.float32) / (1.0 + dual_step)


def coil_kernel(first, count, held, far, passed, outs, *refs):
    values, _, targets, (u_buf, v_buf) = sorted_refs(held, far, passed, outs, refs)
    sides = values[:2]
    weight, col_fwd, even_fwd, odd_fwd, col_bwd, even_bwd, odd_bwd = values[2:9]
    blocks = values[9:9 + count] if values[9].ndim == 3 else [values[9].at[n] for n in range(count)]
    totals, (new_own, *packed, new_all) = targets[:count], targets[count:]
    if packed:
        for n in range(count):
            packed[0][n] = blocks[n][...]
    new_other = new_all.at[first:first + count]
    height, depth = weight.shape
    half = height // 2
    kinds = [(n, c) for n in range(count) for c in (0, 1)]

    def maps(n, c):
        return sides[c][0, first + n, 0], sides[c][0, first + n, 1]

    real, imag = [], []
    for n, c in kinds:
        map_re, map_im = maps(n, c)
        image_re, image_im = blocks[n][0], blocks[n][1]
        real.append(map_re * image_re - map_im * image_im)
        imag.append(map_re * image_im + map_im * image_re)
    lines = columns_dft(jnp.concatenate(real, axis=0), jnp.concatenate(imag, axis=0), col_fwd[...])
    u_buf[0] = lines[:, :depth]
    u_buf[1] = lines[:, depth:]
    halves = []
    for odd, table in ((0, even_fwd), (1, odd_fwd)):
        cells = jnp.concatenate([
            jnp.concatenate([u_buf[part, pl.ds(k * height + odd, half, stride=2), :] for part in (0, 1)], axis=0)
            for k in range(len(kinds))
        ], axis=1)
        halves.append(rows_dft(table[...], cells))
    spectrum = (halves[0] + halves[1], halves[0] - halves[1])
    updated = []
    for q in (0, 1):
        span = pl.ds(q * half, half)
        columns = []
        for k, (n, c) in enumerate(kinds):
            new = (new_own, new_other)[c]
            pieces = []
            for part in (0, 1):
                value = spectrum[q][part * half:(part + 1) * half, k * depth:(k + 1) * depth]
                piece = weight[span, :] * (sides[c][1, first + n, part, span, :] + dual_step * value)
                new[n, part, span, :] = piece
                pieces.append(piece)
            columns.append(jnp.concatenate(pieces, axis=0))
        updated.append(jnp.concatenate(columns, axis=1))
    for odd, table in ((0, even_bwd), (1, odd_bwd)):
        back = rows_dft(table[...], updated[0] - updated[1] if odd else updated[0] + updated[1])
        for k in range(len(kinds)):
            for part in (0, 1):
                v_buf[part, pl.ds(k * height + odd, half, stride=2), :] = back[
                    part * half:(part + 1) * half, k * depth:(k + 1) * depth
                ]
    back = columns_dft(v_buf[0], v_buf[1], col_bwd[...])
    for n in range(count):
        total_re, total_im = 0.0, 0.0
        for c in (0, 1):
            map_re, map_im = maps(n, c)
            rows = slice((2 * n + c) * height, (2 * n + c + 1) * height)
            back_re, back_im = back[rows, :depth], back[rows, depth:]
            total_re = total_re + map_re * back_re + map_im * back_im
            total_im = total_im + map_re * back_im - map_im * back_re
        totals[n][0] = total_re
        totals[n][1] = total_im


def project(moved):
    magnitude = jnp.sqrt(moved[0] * moved[0] + moved[1] * moved[1])
    factor = clip_level / jnp.maximum(magnitude, clip_level)
    return [value * factor for value in moved]


def temporal_kernel(total, held, far, passed, outs, *refs):
    (image, pair, pair_before, *others), _, (tv_new, begin), _ = sorted_refs(held, far, passed, outs, refs)
    current, dual = pair.at[0:2], pair.at[2:4]
    previous, dual_before = pair_before.at[0:2], pair_before.at[2:4]
    later = others[0] if others else previous
    place = placed()
    not_first = jnp.where(place[2] > 0, 1.0, 0.0)
    not_last = jnp.where(place[2] < total - 1, 1.0, 0.0)
    own = project([
        dual[part] + (dual_step * not_last) * (later[part] - current[part]) for part in (0, 1)
    ])
    earlier = project([
        dual_before[part] + dual_step * (current[part] - previous[part]) for part in (0, 1)
    ])
    for part in (0, 1):
        tv_new[part] = own[part]
        begin[part] = image[part] - primal_step * (not_first * earlier[part] - not_last * own[part])


def pass_kernel(held, far, passed, outs, *refs):
    pass


def sum_kernel(begun, held, far, passed, outs, *refs):
    values, _, (target,), _ = sorted_refs(held, far, passed, outs, refs)
    for part in (0, 1):
        total = 0.0
        for value in values[:held - begun]:
            total = total + value[part]
        target[part] = values[-1][part] - primal_step * total if begun else total


def store_kernel(other, count, *refs):
    groups, data_new, sems = refs[:count], refs[-3], refs[-1]
    place = placed()
    stores = []
    for g, group in enumerate(groups):
        for n in range(group.shape[0]):
            offset = g * group.shape[0] + n
            plane = 2 * jnp.bitwise_xor(place[0], offset) + jnp.bitwise_xor(place[1], other)
            stores.append(pltpu.make_async_copy(group.at[n], data_new.at[:, 0, 0, plane], sems.at[offset]))
            stores[-1].start()
    for store in stores:
        store.wait()


def turned(value, axis, steps):
    count = lax.axis_size(axis)
    return lax.ppermute(value, axis, [(source, (source + steps) % count) for source in range(count)])


def swapped(value, mask):
    count = lax.axis_size("space")
    return lax.ppermute(value, "space", [(source, source ^ mask) for source in range(count)])


def on_device(image, extrap, tv_dual, data_dual, kspace, coil_maps, sampling):
    height, depth = kspace.shape[4:]
    chips = lax.axis_size("space") // 2
    inner = chips // 4
    frame_total = lax.axis_size("tm")
    tables = [
        jnp.asarray(table)
        for table in (
            column_table(depth, -1), *row_tables(height, -1), column_table(depth, 1), *row_tables(height, 1)
        )
    ]
    block = pltpu.VMEM((2, height, depth), jnp.float32)
    result = jax.ShapeDtypeStruct((2, height, depth), jnp.float32)

    def ahead(work, token, *values):
        _, (token, *values) = call("ahead", pass_kernel, [], [], [token, *values], [], [], work, 2)
        return (token, *values)

    blocks = {2 * inner: swapped(extrap[:, 0], 4 * inner)}
    for i in range(1, inner):
        blocks[i] = swapped(extrap[:, 0], 2 * i)

    half = pltpu.VMEM((2, chips, 2, height, depth), jnp.float32)
    (*tables, token, weight, image_here, blocks[0], pair, near, give), _ = call(
        "load", load_kernel, [], [*tables, image, extrap, tv_dual, sampling, coil_maps, data_dual, kspace], [],
        [pltpu.VMEM(value.shape, value.dtype) for value in tables]
        + [pltpu.VMEM((8, 128), jnp.float32), pltpu.VMEM((height, depth), jnp.float32)]
        + [block, block, pltpu.VMEM((4, height, depth), jnp.float32), half, half],
        [
            pltpu.VMEM((2, chips, 2, height, depth), jnp.float32),
            pltpu.VMEM((1, height, depth), jnp.int32),
            pltpu.SemaphoreType.DMA((2, chips, 3)),
            pltpu.SemaphoreType.DMA((len(tables) + 5,)),
        ],
        1, 4,
    )
    other = swapped(give, 1)
    pair_before = turned(pair, "tm", 1)
    later = [] if frame_total == 2 else [turned(blocks[0], "tm", -1)]

    def store(name, whose, groups, before, token):
        operands = [pltpu.with_memory_space_constraint(value, pltpu.VMEM) for value in groups]
        operands += [pltpu.with_memory_space_constraint(value, pltpu.HBM) for value in before] + [token]
        return pl.pallas_call(
            functools.partial(store_kernel, whose, len(groups)),
            out_shape=[
                jax.ShapeDtypeStruct(kspace.shape, jnp.float32), jax.ShapeDtypeStruct(token.shape, token.dtype)
            ],
            in_specs=[vmem] * len(groups) + [hbm] * len(before) + [anywhere],
            out_specs=[hbm, anywhere],
            scratch_shapes=[pltpu.SemaphoreType.DMA((chips,))],
            input_output_aliases={len(groups) + n: n for n in (range(2) if before else ())} or {len(groups): 1},
            compiler_params=pltpu.CompilerParams(vmem_limit_bytes=2 * mebi),
            cost_estimate=pl.CostEstimate(flops=1_000, bytes_accessed=100, transcendentals=0),
            name=name,
        )(*operands)

    totals, new_own = {}, {}

    def coils(z, token, arrays, new_other, packs=False):
        held = [near, other, weight, *tables, *arrays, *new_other]
        found, (token,) = call(
            "coils", functools.partial(coil_kernel, z * inner, inner), held, [], [token],
            [block] * inner + [pltpu.VMEM((inner, 2, height, depth), jnp.float32)] * (2 if packs else 1)
            + [pltpu.VMEM((chips, 2, height, depth), jnp.float32)],
            [pltpu.VMEM((2, 2 * inner * height, depth), jnp.float32)] * 2,
            100_000, 8, len(held) - 1 if new_other else None,
        )
        totals[z], new_own[z] = list(found[:inner]), found[inner]
        return (token, found[-1:], *(found[inner + 1:-1]))

    def beside(z):
        return [swapped(totals[z][i], 2 * i) for i in range(1, inner)]

    def sums(values, passed, work):
        (found,), passed = call("sums", functools.partial(sum_kernel, 0), values, [], passed, [block], [], work, 2)
        return (found, *passed)

    token, blocks[2 * inner] = ahead(30_000_000, token, blocks[2 * inner])
    blocks[3 * inner] = swapped(blocks[2 * inner], 2 * inner)
    for i in range(1, inner):
        blocks[2 * inner + i] = swapped(blocks[2 * inner], 2 * i)
    token, new_other, pack = coils(0, token, [blocks[i] for i in range(inner)], [], True)
    pack = swapped(pack, 2 * inner)
    token, blocks[3 * inner] = ahead(1, token, blocks[3 * inner])
    for i in range(1, inner):
        blocks[3 * inner + i] = swapped(blocks[3 * inner], 2 * i)
    for z in (2, 3):
        token, new_other = coils(z, token, [blocks[z * inner + i] for i in range(inner)], new_other)
    beside_far = beside(3)
    token, new_other = coils(1, token, [pack], new_other)
    part, token, *totals[1][1:] = sums([totals[2][0], *beside(2)], [token, *totals[1][1:]], 50)
    from_2 = swapped(part, 4 * inner)
    part, token = sums([totals[3][0], *beside_far], [token], 50)
    from_3 = swapped(part, 6 * inner)
    part, token = sums([totals[1][0], *beside(1)], [token], 50)
    from_1 = swapped(part, 2 * inner)
    (tv_here, begin), (token,) = call(
        "temporal", functools.partial(temporal_kernel, frame_total), [image_here, pair, pair_before, *later], [], [token],
        [result, block], [], 50, 4,
    )
    data_new, token = store("store", 0, [new_own[z] for z in range(4)], [], token)
    total, token = sums([totals[0][0], from_2], [token], 100000)
    total, token = sums([total, from_3], [token], 50000)
    (image_new,), (token,) = call(
        "sums", functools.partial(sum_kernel, 1), [total, from_1, *beside(0), begin], [], [token], [result], [],
        20_000_000, 2,
    )
    data_new, _ = store("store", 1, [swapped(new_other[0], 1)], [data_new], token)
    return (image_new[:, None], tv_here[:, None], data_new)


def passed_along(value, axis, steps):
    count = lax.axis_size(axis)
    initial, last = (max(0, -steps), min(count, count - steps))
    return lax.ppermute(value, axis, [(source, source + steps) for source in range(initial, last)])


def plain_tables(length):
    places = lax.iota(jnp.int32, length)
    product = places[:, None] * places[None, :] % length
    angles = product.astype(jnp.float32) * (2.0 * math.pi / length)
    factor = 1.0 / math.sqrt(length)
    return (jnp.cos(angles) * factor, jnp.sin(angles) * factor)


def right_mult(values, table):
    return jnp.dot(values, table, precision=lax.Precision.HIGHEST, preferred_element_type=jnp.float32)


def left_mult(table, values):
    return jnp.einsum(
        "ky,cxyz->cxkz", table, values, precision=lax.Precision.HIGHEST, preferred_element_type=jnp.float32
    )


def on_any(image, extrap, tv_dual, data_dual, kspace, coil_maps, sampling):
    readout = kspace.shape[3]
    height = kspace.shape[4]
    depth = kspace.shape[5]
    coil_count = kspace.shape[2]
    own_rows = image.shape[2]
    cos_cols, sin_cols = plain_tables(depth)
    cos_rows, sin_rows = plain_tables(height)
    frame_here = lax.axis_index("tm")
    frame_total = lax.axis_size("tm")
    not_last = (frame_here < frame_total - 1).astype(jnp.float32)
    current = extrap[:, 0]
    later = passed_along(current, "tm", -1)
    moved = tv_dual[:, 0] + dual_step * not_last * (later - current)
    tv_real, tv_imag = project(moved)
    tv_here = jnp.stack([tv_real, tv_imag])
    piece = lax.all_gather(current, "space", axis=1, tiled=True)
    piece_real = piece[0][None]
    piece_imag = piece[1][None]
    coil_real = coil_maps[0] * piece_real - coil_maps[1] * piece_imag
    coil_imag = coil_maps[0] * piece_imag + coil_maps[1] * piece_real
    out_real = right_mult(coil_real, cos_cols) + right_mult(coil_imag, sin_cols)
    out_imag = right_mult(coil_imag, cos_cols) - right_mult(coil_real, sin_cols)
    half_spectrum = jnp.stack([out_real, out_imag])
    half_spectrum = half_spectrum.reshape(2, coil_count, readout, height, depth)
    spec_real = left_mult(cos_rows, half_spectrum[0]) + left_mult(sin_rows, half_spectrum[1])
    spec_imag = left_mult(cos_rows, half_spectrum[1]) - left_mult(sin_rows, half_spectrum[0])
    weight = sampling[0].astype(jnp.float32)
    scaled = weight / (1.0 + dual_step)
    dual_real = scaled * (data_dual[0, 0] + dual_step * (spec_real - kspace[0, 0]))
    dual_imag = scaled * (data_dual[1, 0] + dual_step * (spec_imag - kspace[1, 0]))
    back_real = left_mult(cos_rows, dual_real) - left_mult(sin_rows, dual_imag)
    back_imag = left_mult(cos_rows, dual_imag) + left_mult(sin_rows, dual_real)
    back_real = back_real.reshape(coil_count, readout * height, depth)
    back_imag = back_imag.reshape(coil_count, readout * height, depth)
    plane_real = right_mult(back_real, cos_cols) - right_mult(back_imag, sin_cols)
    plane_imag = right_mult(back_imag, cos_cols) + right_mult(back_real, sin_cols)
    term_real = jnp.sum(coil_maps[0] * plane_real + coil_maps[1] * plane_imag, axis=0)
    term_imag = jnp.sum(coil_maps[0] * plane_imag - coil_maps[1] * plane_real, axis=0)
    coil_term = jnp.stack([term_real, term_imag])
    combined = lax.psum(coil_term, "space")
    adjoint = lax.dynamic_slice_in_dim(combined, lax.axis_index("space") * own_rows, own_rows, 1)
    earlier = passed_along(tv_here, "tm", 1)
    temporal = earlier - not_last * tv_here
    image_new = image[:, 0] - primal_step * (adjoint + temporal)
    data_new = jnp.stack([dual_real, dual_imag])[:, None]
    return (image_new[:, None], tv_here[:, None], data_new)


def solution(mesh):
    in_specs = (
        P(None, "tm", "space", None),
        P(None, "tm", "space", None),
        P(None, "tm", "space", None),
        P(None, "tm", "space", None, None, None),
        P(None, "tm", "space", None, None, None),
        P(None, "space", None, None),
        P("tm", None, None),
    )
    out_specs = (
        P(None, "tm", "space", None),
        P(None, "tm", "space", None),
        P(None, "tm", "space", None, None, None),
    )

    def either(*local):
        kspace = local[4]
        one_plane = local[0].shape[2] == kspace.shape[4] and mesh.shape["space"] == kspace.shape[3]
        paired = mesh.shape["space"] % 8 == 0 and mesh.shape["space"] & (mesh.shape["space"] - 1) == 0
        return (on_device if one_plane and paired else on_any)(*local)

    return jax.shard_map(
        either, mesh=mesh, in_specs=in_specs, out_specs=out_specs, check_vma=False
    )
```

```python
import functools
import math

import jax
import jax.numpy as jnp
import ml_dtypes
import numpy as np
from jax import lax
from jax.experimental import pallas as pl
from jax.experimental.pallas import tpu as pltpu
from jax.sharding import PartitionSpec as P

dual_step = 0.4
primal_step = 0.4
clip_level = 0.5


def split_host(table):
    high = table.astype(ml_dtypes.bfloat16)
    low = (table - high.astype(np.float64)).astype(ml_dtypes.bfloat16)
    return high, low


def column_table(length, sign):
    places = np.arange(length)
    angles = 2.0 * math.pi * (np.outer(places, places) % length) / length
    real = np.cos(angles) / math.sqrt(length)
    imag = sign * np.sin(angles) / math.sqrt(length)
    whole = np.block([[real, imag], [-imag, real]])
    high, low = split_host(whole)
    return np.concatenate([high, high, low], axis=0)


def row_tables(length, sign):
    half = length // 2
    found = []
    for odd in (0, 1):
        lines = np.arange(half)
        cells = 2 * np.arange(half) + odd
        product = np.outer(lines, cells)
        angles = 2.0 * math.pi * (product % length) / length
        real = np.cos(angles) / math.sqrt(length)
        imag = sign * np.sin(angles) / math.sqrt(length)
        if sign > 0:
            real, imag = real.T, imag.T
        whole = np.block([[real, -imag], [imag, real]])
        high, low = split_host(whole)
        found.append(np.concatenate([high, high, low], axis=1))
    return found


def split(values):
    high = values.astype(jnp.bfloat16)
    low = (values - high.astype(jnp.float32)).astype(jnp.bfloat16)
    return high, low


def columns_dft(real, imag, table):
    real_high, real_low = split(real)
    imag_high, imag_low = split(imag)
    left = jnp.concatenate([real_high, imag_high, real_low, imag_low, real_high, imag_high], axis=1)
    return jnp.dot(left, table, preferred_element_type=jnp.float32)


def rows_dft(table, values):
    high, low = split(values)
    return jnp.dot(table, jnp.concatenate([high, low, high], axis=0), preferred_element_type=jnp.float32)


vmem = pl.BlockSpec(memory_space=pltpu.VMEM)
hbm = pl.BlockSpec(memory_space=pltpu.HBM)
anywhere = pl.BlockSpec(memory_space=pl.ANY)
mebi = 1024 * 1024


def call(name, kernel, held, far, passed, outs, scratch, work, limit, shared=None):
    operands = [
        *[pltpu.with_memory_space_constraint(value, pltpu.VMEM) for value in held],
        *[pltpu.with_memory_space_constraint(value, pltpu.HBM) for value in far],
    ]
    aliases = {len(operands) + n: len(outs) + n for n in range(len(passed))}
    if shared is not None:
        aliases[shared] = len(outs) - 1
    found = pl.pallas_call(
        functools.partial(kernel, len(held), len(far), len(passed), len(outs)),
        out_shape=list(outs) + [jax.ShapeDtypeStruct(value.shape, value.dtype) for value in passed],
        in_specs=[vmem] * len(held) + [hbm] * len(far) + [anywhere] * len(passed),
        out_specs=[vmem] * len(outs) + [anywhere] * len(passed),
        scratch_shapes=scratch,
        input_output_aliases=aliases,
        compiler_params=pltpu.CompilerParams(vmem_limit_bytes=limit * mebi),
        cost_estimate=pl.CostEstimate(flops=work * 1_000, bytes_accessed=100, transcendentals=0),
        name=name,
    )(*operands, *passed)
    return found[:len(outs)], found[len(outs):]


def sorted_refs(held, far, passed, outs, refs):
    after = held + far + passed
    return refs[:held], refs[held:held + far], refs[after:after + outs], refs[after + outs + passed:]


def placed():
    here = lax.axis_index("space")
    return here // 2, here % 2, lax.axis_index("tm")


def load_kernel(held, far, passed, outs, *refs):
    _, sources, targets, (ksp_buf, mask_buf, sems, small_sems) = sorted_refs(held, far, passed, outs, refs)
    tables = far - 7
    image, extrap, tv_dual, mask, coil, dual, kspace = sources[tables:]
    token, weight, image_out, here, pair, near, give = targets[tables:]
    token[...] = jnp.zeros(token.shape, token.dtype)
    copies = [
        pltpu.make_async_copy(mask, mask_buf, small_sems.at[tables]),
        pltpu.make_async_copy(image.at[:, 0], image_out, small_sems.at[tables + 1]),
        pltpu.make_async_copy(extrap.at[:, 0], here, small_sems.at[tables + 2]),
        pltpu.make_async_copy(extrap.at[:, 0], pair.at[0:2], small_sems.at[tables + 3]),
        pltpu.make_async_copy(tv_dual.at[:, 0], pair.at[2:4], small_sems.at[tables + 4]),
    ]
    copies += [pltpu.make_async_copy(sources[n], targets[n], small_sems.at[n]) for n in range(tables)]
    _, chips, _, height, _ = near.shape
    place = placed()
    loads = []
    for other, target in enumerate((near, give)):
        for offset in range(chips):
            plane = 2 * jnp.bitwise_xor(place[0], offset) + jnp.bitwise_xor(place[1], other)
            rows = pl.ds(pl.multiple_of(plane * height, height), height)
            loads.append([
                pltpu.make_async_copy(dual.at[:, 0, 0, plane], target.at[1, offset], sems.at[other, offset, 0]),
                pltpu.make_async_copy(kspace.at[:, 0, 0, plane], ksp_buf.at[other, offset], sems.at[other, offset, 1]),
                pltpu.make_async_copy(coil.at[:, 0, rows, :], target.at[0, offset], sems.at[other, offset, 2]),
            ])
    for load in loads:
        for copy in load:
            copy.start()
    for copy in copies:
        copy.start()
    for other, target in enumerate((near, give)):
        for offset in range(chips):
            for copy in loads[other * chips + offset]:
                copy.wait()
            for part in (0, 1):
                target[1, offset, part] = target[1, offset, part] - dual_step * ksp_buf[other, offset, part]
    for copy in copies:
        copy.wait()
    weight[...] = mask_buf[0].astype(jnp.float32) / (1.0 + dual_step)


def coil_kernel(first, count, held, far, passed, outs, *refs):
    values, _, targets, (u_buf, v_buf) = sorted_refs(held, far, passed, outs, refs)
    sides = values[:2]
    weight, col_fwd, even_fwd, odd_fwd, col_bwd, even_bwd, odd_bwd = values[2:9]
    blocks = values[9:9 + count] if values[9].ndim == 3 else [values[9].at[n] for n in range(count)]
    totals, (new_own, *packed, new_all) = targets[:count], targets[count:]
    if packed:
        for n in range(count):
            packed[0][n] = blocks[n][...]
    new_other = new_all.at[first:first + count]
    height, depth = weight.shape
    half = height // 2
    kinds = [(n, c) for n in range(count) for c in (0, 1)]

    def maps(n, c):
        return sides[c][0, first + n, 0], sides[c][0, first + n, 1]

    real, imag = [], []
    for n, c in kinds:
        map_re, map_im = maps(n, c)
        image_re, image_im = blocks[n][0], blocks[n][1]
        real.append(map_re * image_re - map_im * image_im)
        imag.append(map_re * image_im + map_im * image_re)
    lines = columns_dft(jnp.concatenate(real, axis=0), jnp.concatenate(imag, axis=0), col_fwd[...])
    u_buf[0] = lines[:, :depth]
    u_buf[1] = lines[:, depth:]
    halves = []
    for odd, table in ((0, even_fwd), (1, odd_fwd)):
        cells = jnp.concatenate([
            jnp.concatenate([u_buf[part, pl.ds(k * height + odd, half, stride=2), :] for part in (0, 1)], axis=0)
            for k in range(len(kinds))
        ], axis=1)
        halves.append(rows_dft(table[...], cells))
    spectrum = (halves[0] + halves[1], halves[0] - halves[1])
    updated = []
    for q in (0, 1):
        span = pl.ds(q * half, half)
        columns = []
        for k, (n, c) in enumerate(kinds):
            new = (new_own, new_other)[c]
            pieces = []
            for part in (0, 1):
                value = spectrum[q][part * half:(part + 1) * half, k * depth:(k + 1) * depth]
                piece = weight[span, :] * (sides[c][1, first + n, part, span, :] + dual_step * value)
                new[n, part, span, :] = piece
                pieces.append(piece)
            columns.append(jnp.concatenate(pieces, axis=0))
        updated.append(jnp.concatenate(columns, axis=1))
    for odd, table in ((0, even_bwd), (1, odd_bwd)):
        back = rows_dft(table[...], updated[0] - updated[1] if odd else updated[0] + updated[1])
        for k in range(len(kinds)):
            for part in (0, 1):
                v_buf[part, pl.ds(k * height + odd, half, stride=2), :] = back[
                    part * half:(part + 1) * half, k * depth:(k + 1) * depth
                ]
    back = columns_dft(v_buf[0], v_buf[1], col_bwd[...])
    for n in range(count):
        total_re, total_im = 0.0, 0.0
        for c in (0, 1):
            map_re, map_im = maps(n, c)
            rows = slice((2 * n + c) * height, (2 * n + c + 1) * height)
            back_re, back_im = back[rows, :depth], back[rows, depth:]
            total_re = total_re + map_re * back_re + map_im * back_im
            total_im = total_im + map_re * back_im - map_im * back_re
        totals[n][0] = total_re
        totals[n][1] = total_im


def project(moved):
    magnitude = jnp.sqrt(moved[0] * moved[0] + moved[1] * moved[1])
    factor = clip_level / jnp.maximum(magnitude, clip_level)
    return [value * factor for value in moved]


def temporal_kernel(total, held, far, passed, outs, *refs):
    (image, pair, pair_before, *others), _, (tv_new, begin), _ = sorted_refs(held, far, passed, outs, refs)
    current, dual = pair.at[0:2], pair.at[2:4]
    previous, dual_before = pair_before.at[0:2], pair_before.at[2:4]
    later = others[0] if others else previous
    place = placed()
    not_first = jnp.where(place[2] > 0, 1.0, 0.0)
    not_last = jnp.where(place[2] < total - 1, 1.0, 0.0)
    own = project([
        dual[part] + (dual_step * not_last) * (later[part] - current[part]) for part in (0, 1)
    ])
    earlier = project([
        dual_before[part] + dual_step * (current[part] - previous[part]) for part in (0, 1)
    ])
    for part in (0, 1):
        tv_new[part] = own[part]
        begin[part] = image[part] - primal_step * (not_first * earlier[part] - not_last * own[part])


def pass_kernel(held, far, passed, outs, *refs):
    pass


def sum_kernel(begun, held, far, passed, outs, *refs):
    values, _, (target,), _ = sorted_refs(held, far, passed, outs, refs)
    for part in (0, 1):
        total = 0.0
        for value in values[:held - begun]:
            total = total + value[part]
        target[part] = values[-1][part] - primal_step * total if begun else total


def store_kernel(other, count, extra, *refs):
    groups, values = refs[:count], refs[len(refs) - 3 - 2 * extra:len(refs) - 3 - extra]
    data_new, targets, sems = refs[-3 - extra], refs[-1 - extra:-1], refs[-1]
    place = placed()
    stores = [
        pltpu.make_async_copy(value, target, sems.at[sems.shape[0] - 1 - n])
        for n, (value, target) in enumerate(zip(values, targets))
    ]
    for g, group in enumerate(groups):
        for n in range(group.shape[0]):
            offset = g * group.shape[0] + n
            plane = 2 * jnp.bitwise_xor(place[0], offset) + jnp.bitwise_xor(place[1], other)
            stores.append(pltpu.make_async_copy(group.at[n], data_new.at[:, 0, 0, plane], sems.at[offset]))
    for store in stores:
        store.start()
    for store in stores:
        store.wait()


def turned(value, axis, steps):
    count = lax.axis_size(axis)
    return lax.ppermute(value, axis, [(source, (source + steps) % count) for source in range(count)])


def swapped(value, mask):
    count = lax.axis_size("space")
    return lax.ppermute(value, "space", [(source, source ^ mask) for source in range(count)])


def on_device(image, extrap, tv_dual, data_dual, kspace, coil_maps, sampling):
    height, depth = kspace.shape[4:]
    chips = lax.axis_size("space") // 2
    inner = chips // 4
    frame_total = lax.axis_size("tm")
    tables = [
        jnp.asarray(table)
        for table in (
            column_table(depth, -1), *row_tables(height, -1), column_table(depth, 1), *row_tables(height, 1)
        )
    ]
    block = pltpu.VMEM((2, height, depth), jnp.float32)
    result = jax.ShapeDtypeStruct((2, height, depth), jnp.float32)

    def ahead(work, token, *values):
        _, (token, *values) = call("ahead", pass_kernel, [], [], [token, *values], [], [], work, 2)
        return (token, *values)

    blocks = {2 * inner: swapped(extrap[:, 0], 4 * inner)}
    for i in range(1, inner):
        blocks[i] = swapped(extrap[:, 0], 2 * i)

    half = pltpu.VMEM((2, chips, 2, height, depth), jnp.float32)
    (*tables, token, weight, image_here, blocks[0], pair, near, give), _ = call(
        "load", load_kernel, [], [*tables, image, extrap, tv_dual, sampling, coil_maps, data_dual, kspace], [],
        [pltpu.VMEM(value.shape, value.dtype) for value in tables]
        + [pltpu.VMEM((8, 128), jnp.float32), pltpu.VMEM((height, depth), jnp.float32)]
        + [block, block, pltpu.VMEM((4, height, depth), jnp.float32), half, half],
        [
            pltpu.VMEM((2, chips, 2, height, depth), jnp.float32),
            pltpu.VMEM((1, height, depth), jnp.int32),
            pltpu.SemaphoreType.DMA((2, chips, 3)),
            pltpu.SemaphoreType.DMA((len(tables) + 5,)),
        ],
        1, 4,
    )
    other = swapped(give, 1)
    pair_before = turned(pair, "tm", 1)
    later = [] if frame_total == 2 else [turned(blocks[0], "tm", -1)]

    def store(name, whose, groups, before, token, *extra):
        operands = [pltpu.with_memory_space_constraint(value, pltpu.VMEM) for value in groups]
        operands += [pltpu.with_memory_space_constraint(value, pltpu.HBM) for value in before] + [token]
        operands += [pltpu.with_memory_space_constraint(value, pltpu.VMEM) for value in extra]
        return pl.pallas_call(
            functools.partial(store_kernel, whose, len(groups), len(extra)),
            out_shape=[
                jax.ShapeDtypeStruct(kspace.shape, jnp.float32), jax.ShapeDtypeStruct(token.shape, token.dtype)
            ] + [jax.ShapeDtypeStruct(value.shape, value.dtype) for value in extra],
            in_specs=[vmem] * len(groups) + [hbm] * len(before) + [anywhere] + [vmem] * len(extra),
            out_specs=[hbm, anywhere] + [hbm] * len(extra),
            scratch_shapes=[pltpu.SemaphoreType.DMA((chips + len(extra),))],
            input_output_aliases={len(groups) + n: n for n in (range(2) if before else ())} or {len(groups): 1},
            compiler_params=pltpu.CompilerParams(vmem_limit_bytes=2 * mebi),
            cost_estimate=pl.CostEstimate(flops=1_000, bytes_accessed=100, transcendentals=0),
            name=name,
        )(*operands)

    totals, new_own = {}, {}

    def coils(z, token, arrays, new_other, packs=False):
        held = [near, other, weight, *tables, *arrays, *new_other]
        found, (token,) = call(
            "coils", functools.partial(coil_kernel, z * inner, inner), held, [], [token],
            [block] * inner + [pltpu.VMEM((inner, 2, height, depth), jnp.float32)] * (2 if packs else 1)
            + [pltpu.VMEM((chips, 2, height, depth), jnp.float32)],
            [pltpu.VMEM((2, 2 * inner * height, depth), jnp.float32)] * 2,
            100_000, 8, len(held) - 1 if new_other else None,
        )
        totals[z], new_own[z] = list(found[:inner]), found[inner]
        return (token, found[-1:], *(found[inner + 1:-1]))

    def beside(z):
        return [swapped(totals[z][i], 2 * i) for i in range(1, inner)]

    def sums(values, passed, work):
        (found,), passed = call("sums", functools.partial(sum_kernel, 0), values, [], passed, [block], [], work, 2)
        return (found, *passed)

    token, blocks[2 * inner] = ahead(30_000_000, token, blocks[2 * inner])
    blocks[3 * inner] = swapped(blocks[2 * inner], 2 * inner)
    for i in range(1, inner):
        blocks[2 * inner + i] = swapped(blocks[2 * inner], 2 * i)
    token, new_other, pack = coils(0, token, [blocks[i] for i in range(inner)], [], True)
    pack = swapped(pack, 2 * inner)
    token, blocks[3 * inner] = ahead(1, token, blocks[3 * inner])
    for i in range(1, inner):
        blocks[3 * inner + i] = swapped(blocks[3 * inner], 2 * i)
    for z in (2, 3):
        token, new_other = coils(z, token, [blocks[z * inner + i] for i in range(inner)], new_other)
    beside_far = beside(3)
    token, new_other = coils(1, token, [pack], new_other)
    part, token, *totals[1][1:] = sums([totals[2][0], *beside(2)], [token, *totals[1][1:]], 50)
    from_2 = swapped(part, 4 * inner)
    part, token = sums([totals[3][0], *beside_far], [token], 50)
    from_3 = swapped(part, 6 * inner)
    part, token = sums([totals[1][0], *beside(1)], [token], 50)
    from_1 = swapped(part, 2 * inner)
    (tv_here, begin), (token,) = call(
        "temporal", functools.partial(temporal_kernel, frame_total), [image_here, pair, pair_before, *later], [], [token],
        [result, block], [], 50, 4,
    )
    data_new, token = store("store", 0, [new_own[z] for z in range(4)], [], token)
    total, token = sums([totals[0][0], from_2], [token], 100000)
    total, token = sums([total, from_3], [token], 50000)
    (image_new,), (token,) = call(
        "sums", functools.partial(sum_kernel, 1), [total, from_1, *beside(0), begin], [], [token], [block], [],
        20_000_000, 2,
    )
    data_new, _, image_new = store("store", 1, [swapped(new_other[0], 1)], [data_new], token, image_new)
    return (image_new[:, None], tv_here[:, None], data_new)


def passed_along(value, axis, steps):
    count = lax.axis_size(axis)
    initial, last = (max(0, -steps), min(count, count - steps))
    return lax.ppermute(value, axis, [(source, source + steps) for source in range(initial, last)])


def plain_tables(length):
    places = lax.iota(jnp.int32, length)
    product = places[:, None] * places[None, :] % length
    angles = product.astype(jnp.float32) * (2.0 * math.pi / length)
    factor = 1.0 / math.sqrt(length)
    return (jnp.cos(angles) * factor, jnp.sin(angles) * factor)


def right_mult(values, table):
    return jnp.dot(values, table, precision=lax.Precision.HIGHEST, preferred_element_type=jnp.float32)


def left_mult(table, values):
    return jnp.einsum(
        "ky,cxyz->cxkz", table, values, precision=lax.Precision.HIGHEST, preferred_element_type=jnp.float32
    )


def on_any(image, extrap, tv_dual, data_dual, kspace, coil_maps, sampling):
    readout = kspace.shape[3]
    height = kspace.shape[4]
    depth = kspace.shape[5]
    coil_count = kspace.shape[2]
    own_rows = image.shape[2]
    cos_cols, sin_cols = plain_tables(depth)
    cos_rows, sin_rows = plain_tables(height)
    frame_here = lax.axis_index("tm")
    frame_total = lax.axis_size("tm")
    not_last = (frame_here < frame_total - 1).astype(jnp.float32)
    current = extrap[:, 0]
    later = passed_along(current, "tm", -1)
    moved = tv_dual[:, 0] + dual_step * not_last * (later - current)
    tv_real, tv_imag = project(moved)
    tv_here = jnp.stack([tv_real, tv_imag])
    piece = lax.all_gather(current, "space", axis=1, tiled=True)
    piece_real = piece[0][None]
    piece_imag = piece[1][None]
    coil_real = coil_maps[0] * piece_real - coil_maps[1] * piece_imag
    coil_imag = coil_maps[0] * piece_imag + coil_maps[1] * piece_real
    out_real = right_mult(coil_real, cos_cols) + right_mult(coil_imag, sin_cols)
    out_imag = right_mult(coil_imag, cos_cols) - right_mult(coil_real, sin_cols)
    half_spectrum = jnp.stack([out_real, out_imag])
    half_spectrum = half_spectrum.reshape(2, coil_count, readout, height, depth)
    spec_real = left_mult(cos_rows, half_spectrum[0]) + left_mult(sin_rows, half_spectrum[1])
    spec_imag = left_mult(cos_rows, half_spectrum[1]) - left_mult(sin_rows, half_spectrum[0])
    weight = sampling[0].astype(jnp.float32)
    scaled = weight / (1.0 + dual_step)
    dual_real = scaled * (data_dual[0, 0] + dual_step * (spec_real - kspace[0, 0]))
    dual_imag = scaled * (data_dual[1, 0] + dual_step * (spec_imag - kspace[1, 0]))
    back_real = left_mult(cos_rows, dual_real) - left_mult(sin_rows, dual_imag)
    back_imag = left_mult(cos_rows, dual_imag) + left_mult(sin_rows, dual_real)
    back_real = back_real.reshape(coil_count, readout * height, depth)
    back_imag = back_imag.reshape(coil_count, readout * height, depth)
    plane_real = right_mult(back_real, cos_cols) - right_mult(back_imag, sin_cols)
    plane_imag = right_mult(back_imag, cos_cols) + right_mult(back_real, sin_cols)
    term_real = jnp.sum(coil_maps[0] * plane_real + coil_maps[1] * plane_imag, axis=0)
    term_imag = jnp.sum(coil_maps[0] * plane_imag - coil_maps[1] * plane_real, axis=0)
    coil_term = jnp.stack([term_real, term_imag])
    combined = lax.psum(coil_term, "space")
    adjoint = lax.dynamic_slice_in_dim(combined, lax.axis_index("space") * own_rows, own_rows, 1)
    earlier = passed_along(tv_here, "tm", 1)
    temporal = earlier - not_last * tv_here
    image_new = image[:, 0] - primal_step * (adjoint + temporal)
    data_new = jnp.stack([dual_real, dual_imag])[:, None]
    return (image_new[:, None], tv_here[:, None], data_new)


def solution(mesh):
    in_specs = (
        P(None, "tm", "space", None),
        P(None, "tm", "space", None),
        P(None, "tm", "space", None),
        P(None, "tm", "space", None, None, None),
        P(None, "tm", "space", None, None, None),
        P(None, "space", None, None),
        P("tm", None, None),
    )
    out_specs = (
        P(None, "tm", "space", None),
        P(None, "tm", "space", None),
        P(None, "tm", "space", None, None, None),
    )

    def either(*local):
        kspace = local[4]
        one_plane = local[0].shape[2] == kspace.shape[4] and mesh.shape["space"] == kspace.shape[3]
        paired = mesh.shape["space"] % 8 == 0 and mesh.shape["space"] & (mesh.shape["space"] - 1) == 0
        return (on_device if one_plane and paired else on_any)(*local)

    return jax.shard_map(
        either, mesh=mesh, in_specs=in_specs, out_specs=out_specs, check_vma=False
    )
```
